512 devices in a mesh: dp: 4 (over y), mp: 128 (over z, x, core).
Axes of the slice: x: 4, y: 4, z: 16, core: 2. Of those that a mesh axis runs over, the one named last changes fastest.
Arguments:
- tokens: bfloat16 [512, 8192], P(('dp', 'mp')), may hold values from -6 to 6
- counts: int32 [4], P('dp'), may hold values from 1 to 128, 320 in all
- up_blocks: bfloat16 [2048, 128, 128], P('mp'), may hold values from -0.125 to 0.125
- up_cols: int32 [128, 16], P('mp'), may hold values from 0 to 63, all different within a row
- down_blocks: bfloat16 [2048, 128, 128], P('mp'), may hold values from -0.09375 to 0.09375
- down_rows: int32 [128, 16], P('mp'), may hold values from 0 to 63, all different within a row
- cotangent: bfloat16 [512, 8192], P(('dp', 'mp')), may hold values from -6 to 6
- up_moment: bfloat16 [2048, 128, 128], P('mp'), may hold values from -1 to 1
- up_moment_scale: float32 [2048, 8], P('mp'), may hold values from 0.0005 to 0.005
- up_second: bfloat16 [2048, 128, 128], P('mp'), may hold values from 0.049804688 to 1
- up_second_scale: float32 [2048, 8], P('mp'), may hold values from 1e-06 to 1e-05
- down_moment: bfloat16 [2048, 128, 128], P('mp'), may hold values from -1 to 1
- down_moment_scale: float32 [2048, 8], P('mp'), may hold values from 0.0005 to 0.005
- down_second: bfloat16 [2048, 128, 128], P('mp'), may hold values from 0.049804688 to 1
- down_second_scale: float32 [2048, 8], P('mp'), may hold values from 1e-06 to 1e-05
Outputs:
- layer_output: bfloat16 [512, 8192], P(('dp', 'mp'))
- new_up_blocks: bfloat16 [2048, 128, 128], P('mp')
- new_up_moment: bfloat16 [2048, 128, 128], P('mp')
- new_up_moment_scale: float32 [2048, 8], P('mp')
- new_up_second: bfloat16 [2048, 128, 128], P('mp')
- new_up_second_scale: float32 [2048, 8], P('mp')
- new_down_blocks: bfloat16 [2048, 128, 128], P('mp')
- new_down_moment: bfloat16 [2048, 128, 128], P('mp')
- new_down_moment_scale: float32 [2048, 8], P('mp')
- new_down_second: bfloat16 [2048, 128, 128], P('mp')
- new_down_second_scale: float32 [2048, 8], P('mp')
The draws below stay inside these ranges and needn't reach their ends.
Inputs may be any that keep to these rules, and one draw needn't show every extreme that they name: Each row of up_cols lists 16 different input column blocks; every column block appears somewhere. Each row of down_rows lists 16 different output row blocks; every row block appears somewhere. The first counts[r] token slots of replica r are valid; some replica is full.
All inputs are finite; a program needn't handle non-finite values. Where the reference program divides by a largest or mean magnitude, that divisor is 1e-20 or more. No bound on the sum of `counts` on one device may be relied on, other than what follows from the above.
Results may differ from the reference program's by a relative error of at most 0.0057.
Values may be sent and summed in bfloat16 or wider, within the bound.
A program may use at most 64 MiB of HBM per device.

```python
import math
import jax
import jax.numpy as jnp
import numpy as np
from jax import lax

D = 8192
BLK = 128
QGROUP = 2048
TOK_DEV = 128
K_UP = 16
K_DOWN = 16
GROUPS = 8
TOKENS = 512
N_DP = 4
N_MP = 128


def block_scale(stream_key, shape, split, least, largest):
    def one(dim, shards_of):
        steps = jax.random.uniform(jax.random.fold_in(jax.random.fold_in(stream_key, 6), dim), (shards_of,), jnp.float32, least / len(split), largest / len(split))
        return jnp.repeat(jnp.exp(steps), shape[dim] // shards_of).reshape((-1,) + (1,) * (len(shape) - dim - 1))

    loudness = one(*split[0])
    for cut in split[1:]:
        loudness = loudness * one(*cut)
    return loudness


def picks_of(stream_key, rows, amount, top, lift):
    order = jax.random.permutation(jax.random.fold_in(stream_key, 1), amount)
    favour = order
    for power in range(3):
        favour = favour * favour // amount
    favour = favour * lift // amount
    lots = jax.random.randint(jax.random.fold_in(stream_key, 2), (rows, amount), 0, 4096) + favour
    fixed_rows = jax.random.permutation(jax.random.fold_in(stream_key, 3), rows)[jnp.arange(amount) % rows]
    lots = jnp.where(jnp.arange(rows)[:, None] == fixed_rows[None, :], 1 << 14, lots)
    priority = lots * amount + jnp.arange(amount)
    return lax.top_k(priority.astype(jnp.int32), top)[1].astype(jnp.int32)


def split_up(amount, total, most, slope):
    weights = [(1 << 20) // math.isqrt(grade ** slope) + 1 for grade in range(2, amount + 1)]
    spare, given = total - most - (amount - 1), [1] * (amount - 1)
    while spare > 0:
        candidates = [i for i in range(amount - 1) if given[i] < most]
        mass, left = sum([weights[i] for i in candidates]), spare
        for i in candidates:
            addition = min(most - given[i], max(1, left * weights[i] // mass), spare)
            given[i] = given[i] + addition
            spare = spare - addition
    return np.array([most] + given)


def ragged(stream_key, amount, total, limit, slope):
    if amount == 2:
        one = jax.random.randint(stream_key, (), max(1, total - limit), min(limit, total - 1) + 1)
        return jnp.stack([one, total - one])
    lengths = jnp.asarray(split_up(amount, total, limit, slope), jnp.int32)
    couples = (amount - 1) // 2
    donor, taker = lengths[1:1 + 2 * couples:2], lengths[2:2 + 2 * couples:2]
    room = jnp.minimum(donor - 1, limit - taker)
    shifted = jax.random.randint(jax.random.fold_in(stream_key, 1), (couples,), 0, 1 << 20) % (room + 1)
    lengths = lengths.at[1:1 + 2 * couples:2].set(donor - shifted).at[2:2 + 2 * couples:2].set(taker + shifted)
    return lengths[jax.random.permutation(jax.random.fold_in(stream_key, 2), amount)]


def scatter_about(own_key, shape, width, bound, cuts=(), kind=jnp.bfloat16):
    drawn = jax.random.normal(own_key, shape, jnp.float32) * width
    if len(cuts) > 0:
        drawn = block_scale(own_key, shape, cuts, -0.22, 0.18) * drawn
    return jnp.clip(drawn, min=-bound, max=bound).astype(kind)


def setup_inputs(seed: int = 0) -> dict:
    keys = jax.random.split(jax.random.key(seed), 16)
    return {
        "tokens": scatter_about(keys[0], (TOKENS, D), 1.0, 6.0, ((0, 512),)),
        "counts": ragged(keys[1], N_DP, TOK_DEV * N_DP * 5 // 8, TOK_DEV, 2).astype(jnp.int32),
        "up_blocks": scatter_about(keys[2], (N_MP * K_UP, BLK, BLK), (K_UP * BLK) ** -0.5, 0.125, ((0, 128),)),
        "up_cols": picks_of(keys[3], N_MP, D // BLK, K_UP, 2048),
        "down_blocks": scatter_about(keys[4], (N_MP * K_DOWN, BLK, BLK), (N_MP * BLK // 4) ** -0.5, 0.09375, ((0, 128),)),
        "down_rows": picks_of(keys[5], N_MP, D // BLK, K_DOWN, 2048),
        "cotangent": scatter_about(keys[6], (TOKENS, D), 1.0, 6.0, ((0, 512),)),
        "up_moment": jnp.clip(jax.random.uniform(keys[7], (N_MP * K_UP, BLK, BLK), jnp.float32, -1.0, 1.0) * block_scale(keys[7], (N_MP * K_UP, BLK, BLK), ((0, 128),), -0.4, 0.0), -1.0, 1.0).astype(jnp.bfloat16),
        "up_moment_scale": jnp.clip(jnp.exp(math.log(0.005) - 2.30258502 * jax.random.uniform(keys[8], (N_MP * K_UP, GROUPS), jnp.float32) ** block_scale(keys[8], (N_MP * K_UP, GROUPS), ((0, 128),), -0.2, 0.2)), 0.0005, 0.005),
        "up_second": jnp.clip(0.049804688 + 0.9501953 * jax.random.uniform(keys[9], (N_MP * K_UP, BLK, BLK), jnp.float32) ** block_scale(keys[9], (N_MP * K_UP, BLK, BLK), ((0, 128),), -0.2, 0.2), 0.049804688, 1.0).astype(jnp.bfloat16),
        "up_second_scale": jnp.clip(jnp.exp(math.log(9.999999747378752e-06) - 2.3025851 * jax.random.uniform(keys[10], (N_MP * K_UP, GROUPS), jnp.float32) ** block_scale(keys[10], (N_MP * K_UP, GROUPS), ((0, 128),), -0.2, 0.2)), 9.999999974752427e-07, 9.999999747378752e-06),
        "down_moment": jnp.clip(jax.random.uniform(keys[11], (N_MP * K_DOWN, BLK, BLK), jnp.float32, -1.0, 1.0) * block_scale(keys[11], (N_MP * K_DOWN, BLK, BLK), ((0, 128),), -0.4, 0.0), -1.0, 1.0).astype(jnp.bfloat16),
        "down_moment_scale": jnp.clip(jnp.exp(math.log(0.005) - 2.30258502 * jax.random.uniform(keys[12], (N_MP * K_DOWN, GROUPS), jnp.float32) ** block_scale(keys[12], (N_MP * K_DOWN, GROUPS), ((0, 128),), -0.2, 0.2)), 0.0005, 0.005),
        "down_second": jnp.clip(0.049804688 + 0.9501953 * jax.random.uniform(keys[13], (N_MP * K_DOWN, BLK, BLK), jnp.float32) ** block_scale(keys[13], (N_MP * K_DOWN, BLK, BLK), ((0, 128),), -0.2, 0.2), 0.049804688, 1.0).astype(jnp.bfloat16),
        "down_second_scale": jnp.clip(jnp.exp(math.log(9.999999747378752e-06) - 2.3025851 * jax.random.uniform(keys[14], (N_MP * K_DOWN, GROUPS), jnp.float32) ** block_scale(keys[14], (N_MP * K_DOWN, GROUPS), ((0, 128),), -0.2, 0.2)), 9.999999974752427e-07, 9.999999747378752e-06),
    }


beta_one = 0.9
beta_two = 0.99
learn_rate = 0.002
decay_rate = 0.1
adam_eps = 1e-08
scale_eps = 1e-06
bias_one = 1.0 - 0.9 ** 10
bias_two = 1.0 - 0.99 ** 10

def adam_blocks(weight, gradient, moment, moment_scale, second, second_scale):
    group_shape = (weight.shape[0], moment_scale.shape[1], QGROUP // BLK, BLK)
    grad_groups = gradient.reshape(group_shape)
    moment_old = moment.astype(jnp.float32).reshape(group_shape) * moment_scale[:, :, None, None]
    second_old = second.astype(jnp.float32).reshape(group_shape) * second_scale[:, :, None, None]
    moment_new = beta_one * moment_old + (1.0 - beta_one) * grad_groups
    second_new = beta_two * second_old + (1.0 - beta_two) * grad_groups * grad_groups
    direction = moment_new / bias_one / (jnp.sqrt(second_new / bias_two) + adam_eps)
    weight_old = weight.astype(jnp.float32).reshape(group_shape)
    weight_new = (weight_old - learn_rate * (direction + decay_rate * weight_old)).astype(jnp.bfloat16)
    moment_top = lax.optimization_barrier(jnp.max(jnp.abs(moment_new), axis=(2, 3))) + scale_eps
    second_top = lax.optimization_barrier(jnp.max(second_new, axis=(2, 3))) + scale_eps
    moment_code = (moment_new / moment_top[:, :, None, None]).astype(jnp.bfloat16)
    second_code = (second_new / second_top[:, :, None, None]).astype(jnp.bfloat16)
    return (weight_new.reshape(weight.shape), moment_code.reshape(weight.shape), moment_top, second_code.reshape(weight.shape), second_top)

def reference(tokens, counts, up_blocks, up_cols, down_blocks, down_rows, cotangent, up_moment, up_moment_scale, up_second, up_second_scale, down_moment, down_moment_scale, down_second, down_second_scale):
    col_blocks = D // BLK
    position = jnp.arange(TOKENS, dtype=jnp.int32)
    valid_rows = (position % TOK_DEV < counts[position // TOK_DEV]).astype(jnp.bfloat16)[:, None]
    token_total = jnp.sum(counts).astype(jnp.float32)
    inputs = tokens.reshape(TOKENS, col_blocks, BLK)
    masked_cot = (cotangent * valid_rows).reshape(TOKENS, col_blocks, BLK)
    up_owned = up_blocks.reshape(N_MP, K_UP, BLK, BLK)
    down_owned = down_blocks.reshape(N_MP, K_DOWN, BLK, BLK)

    def per_owner(partial_out, owner_items):
        up_weight, col_index, down_weight, row_index = owner_items
        picked = jnp.take(inputs, col_index, axis=1).astype(jnp.float32)
        preact = jnp.einsum('tki,koi->to', picked, up_weight.astype(jnp.float32))
        hidden = jax.nn.silu(preact).astype(jnp.bfloat16).astype(jnp.float32)
        contrib = jnp.einsum('ti,koi->tko', hidden, down_weight.astype(jnp.float32))
        partial_out = partial_out.at[:, row_index, :].add(contrib)
        picked_cot = jnp.take(masked_cot, row_index, axis=1).astype(jnp.float32)
        hidden_grad = jnp.einsum('tko,koi->ti', picked_cot, down_weight.astype(jnp.float32))
        down_grad = jnp.einsum('tko,ti->koi', picked_cot, hidden)
        squash = jax.nn.sigmoid(preact)
        pre_grad = (hidden_grad * squash * (1.0 + preact * (1.0 - squash))).astype(jnp.bfloat16)
        up_grad = jnp.einsum('to,tki->koi', pre_grad.astype(jnp.float32), picked)
        return (partial_out, (up_grad, down_grad))
    empty_sum = jnp.zeros((TOKENS, col_blocks, BLK), jnp.float32)
    summed, grads = lax.scan(per_owner, empty_sum, (up_owned, up_cols, down_owned, down_rows))
    layer_output = (summed.reshape(TOKENS, D) * valid_rows.astype(jnp.float32)).astype(jnp.bfloat16)
    up_grad = grads[0].reshape(N_MP * K_UP, BLK, BLK) / token_total
    down_grad = grads[1].reshape(N_MP * K_DOWN, BLK, BLK) / token_total
    up_new = adam_blocks(up_blocks, up_grad, up_moment, up_moment_scale, up_second, up_second_scale)
    down_new = adam_blocks(down_blocks, down_grad, down_moment, down_moment_scale, down_second, down_second_scale)
    return (layer_output, up_new[0], up_new[1], up_new[2], up_new[3], up_new[4], down_new[0], down_new[1], down_new[2], down_new[3], down_new[4])
```

```python
import functools

import jax
import jax.numpy as jnp
from jax import lax
from jax.experimental import pallas as pl
from jax.experimental.pallas import tpu as pltpu
from jax.sharding import PartitionSpec as P

D = 8192
BLK = 128
COLS = D // BLK
K = 16
NZ = 16
NS = 8
NY = 4
ROWS = 128
QROWS = 16
CODE_TOP = 32767.0

beta_one = 0.9
beta_two = 0.99
learn_rate = 0.002
decay_rate = 0.1
adam_eps = 1e-08
scale_eps = 1e-06
bias_one = 1.0 - 0.9**10
bias_two = 1.0 - 0.99**10

MESH = pl.DeviceIdType.MESH
F32 = jnp.float32
BF16 = jnp.bfloat16


def exchange_kernel(
    tokens_hbm,
    cot_hbm,
    counts_ref,
    cols_ref,
    rows_ref,
    up_hbm,
    down_hbm,
    layer_ref,
    grad_hbm,
    gscale_hbm,
    tokens_ref,
    cot_ref,
    up_v,
    down_v,
    zbuf,
    rowtmp,
    turned,
    idx_v,
    idx_y,
    idx_s,
    pack,
    picked,
    cbuf,
    rs_recv,
    acc,
    zsend,
    zrecv,
    gbuf,
    gscale,
    grecv,
    gscale_in,
    gsum,
    gsum_scale,
    w_sem,
    i_sem,
    o_sem,
    zs_sem,
    zr_sem,
    is_sem,
    ir_sem,
    ys_sem,
    yr_sem,
    ps_sem,
    pr_sem,
    cs_sem,
    cr_sem,
    fs_sem,
    fr_sem,
    gs_sem,
    gr_sem,
    hs_sem,
    hr_sem,
):
    y = lax.axis_index("dp")
    mp = lax.axis_index("mp")
    z = mp // NS
    s = mp % NS

    def at_z(p):
        return (y, p * NS + s)

    def at_s(p):
        return (y, z * NS + p)

    def at_y(p):
        return (p, mp)

    def off(a, d, n):
        return (a + (d % n)) % n

    def remote(src, dst, ssem, rsem, dev):
        return pltpu.make_async_remote_copy(
            src_ref=src, dst_ref=dst, send_sem=ssem, recv_sem=rsem, device_id=dev, device_id_type=MESH
        )

    barrier = pltpu.get_barrier_semaphore()
    for d in range(1, NZ):
        pl.semaphore_signal(barrier, inc=1, device_id=at_z(off(z, d, NZ)), device_id_type=MESH)
    for d in range(1, NS):
        pl.semaphore_signal(barrier, inc=1, device_id=at_s(off(s, d, NS)), device_id_type=MESH)
    for d in range(1, NY):
        pl.semaphore_signal(barrier, inc=1, device_id=at_y(off(y, d, NY)), device_id_type=MESH)

    load_up = pltpu.make_async_copy(up_hbm, up_v, w_sem.at[0])
    load_down = pltpu.make_async_copy(down_hbm, down_v, w_sem.at[1])
    load_tokens = pltpu.make_async_copy(tokens_hbm, tokens_ref, w_sem.at[2])
    load_cot = pltpu.make_async_copy(cot_hbm, cot_ref, w_sem.at[3])
    load_tokens.start()
    load_cot.start()
    load_up.start()
    load_down.start()

    valid = jnp.clip(counts_ref[0] - mp, 0, 1).astype(F32)

    load_tokens.wait()
    load_cot.wait()
    for m, ref in enumerate((tokens_ref, cot_ref)):
        for i in range(COLS):
            rowtmp[m * COLS + i : m * COLS + i + 1, :] = ref[0:1, i * BLK : (i + 1) * BLK].astype(F32)
    zbuf[z, 0:COLS, :] = rowtmp[0:COLS, :].astype(BF16)
    zbuf[z, COLS : 2 * COLS, :] = (rowtmp[COLS : 2 * COLS, :] * valid).astype(BF16)

    sub = lax.broadcasted_iota(jnp.int32, (8, BLK), 0)
    lane = lax.broadcasted_iota(jnp.int32, (8, BLK), 1)
    tile = jnp.where(sub == 2, K, 0)
    for k in range(K):
        tile = jnp.where((sub == 0) & (lane == k), cols_ref[0, k], tile)
        tile = jnp.where((sub == 1) & (lane == k), rows_ref[0, k], tile)
        tile = jnp.where((sub == 2) & (lane == rows_ref[0, k]), k, tile)
    tile = jnp.where(sub == 3, counts_ref[0], tile)
    idx_v[s] = tile
    idx_y[0] = tile
    gscale[...] = jnp.zeros_like(gscale)
    gsum_scale[...] = jnp.zeros_like(gsum_scale)
    for src in range(NS):
        rs_recv[src, K] = jnp.zeros((QROWS, BLK), BF16)

    pl.semaphore_wait(barrier, NZ + NS + NY - 3)

    def z_copy(m, w, p, o):
        part = zbuf.at[w, pl.ds(m * COLS, COLS), :]
        return remote(part, part, zs_sem.at[m, o], zr_sem.at[m, o], at_z(p))

    def z_start(m, h, e):
        z_copy(m, off(z, -h, NZ), off(z, e, NZ), (-h - e) % NZ).start()

    def z_wait(m, o):
        z_copy(m, off(z, o, NZ), off(z, 1, NZ), o).wait_recv()

    far = (8, 4, -4)
    near = ((2, 1, -1), (-2, 1, -1))

    for e in far:
        z_start(0, 0, e)
    for d in range(1, NS):
        remote(idx_v.at[s], idx_v.at[s], is_sem.at[d], ir_sem.at[d], at_s(off(s, d, NS))).start()
    for d in range(1, NY):
        remote(idx_y.at[0], idx_y.at[d], ys_sem.at[d], yr_sem.at[d], at_y(off(y, d, NY))).start()
    for e in near[0]:
        z_start(0, 0, e)
    for e in far:
        z_start(1, 0, e)
    for h in (4, -4, 8):
        z_wait(0, (-h) % NZ)
        for e in near[0]:
            z_start(0, h, e)
    for e in near[1]:
        z_start(1, 0, e)
    for h in (4, -4, 8):
        z_wait(1, (-h) % NZ)
        for e in near[1]:
            z_start(1, h, e)

    for d in range(1, NS):
        p = off(s, -d, NS)
        remote(idx_v.at[p], idx_v.at[p], is_sem.at[d], ir_sem.at[d], at_s(p)).wait_recv()
    to_smem = pltpu.make_async_copy(idx_v, idx_s, i_sem)
    to_smem.start()
    to_smem.wait()

    flat = turned.reshape(2, COLS * NZ, BLK)

    def pack_and_send(m):
        for o in range(1, NZ):
            if o % 4:
                z_wait(m, o)
        for w in range(NZ):
            flat[m, pl.ds(w, COLS, stride=NZ), :] = zbuf[w, m * COLS : (m + 1) * COLS, :].astype(F32)

        def one(i, carry):
            d = (s + i) % NS
            for k in range(K):
                pack[m, i, k] = turned[m, idx_s[d, m, k]].astype(BF16)
            remote(pack.at[m, i], picked.at[m, s], ps_sem.at[m, i], pr_sem.at[m, i], at_s(d)).start()
            return carry

        lax.fori_loop(1, NS, one, 0)
        for k in range(K):
            picked[m, s, k] = turned[m, idx_s[s, m, k]].astype(BF16)

    def wait_picked(m):
        for d in range(1, NS):
            p = off(s, -d, NS)
            remote(pack.at[m, d], picked.at[m, p], ps_sem.at[m, d], pr_sem.at[m, d], at_s(p)).wait_recv()
        return jnp.concatenate([picked[m, :, k].reshape(ROWS, BLK) for k in range(K)], axis=1)

    pack_and_send(0)
    pack_and_send(1)

    load_up.wait()
    load_down.wait()
    a_in = wait_picked(0)
    up_wide = jnp.concatenate([up_v[k] for k in range(K)], axis=1)
    preact = lax.dot_general(a_in, up_wide, (((1,), (1,)), ((), ())), preferred_element_type=F32)
    squash = 1.0 / (1.0 + jnp.exp(-preact))
    hidden = (preact * squash).astype(BF16)
    down_tall = down_v[...].reshape(K * BLK, BLK)
    contrib = lax.dot_general(hidden, down_tall, (((1,), (1,)), ((), ())), preferred_element_type=F32)
    for k in range(K):
        cbuf[:, k] = contrib[:, k * BLK : (k + 1) * BLK].astype(BF16).reshape(NS, QROWS, BLK)
    for d in range(1, NS):
        p = off(s, d, NS)
        remote(
            cbuf.at[p], rs_recv.at[s, pl.ds(0, K)], cs_sem.at[d], cr_sem.at[d], at_s(p)
        ).start()
    rs_recv[s, 0:K] = cbuf[s]

    def coded(grad):
        top = jnp.max(jnp.abs(grad), axis=0, keepdims=True)
        code = jnp.round(grad * (CODE_TOP / jnp.maximum(top, 1e-30)))
        return code.astype(jnp.int32).astype(jnp.int16), top * (1.0 / CODE_TOP)

    def grad_store(m, k, grad):
        code, scale = coded(grad)
        gbuf[m, k] = code
        gscale[m, k // 4, k % 4 : k % 4 + 1, :] = scale

    cot_in = wait_picked(1)
    down_grad = lax.dot_general(cot_in, hidden, (((0,), (0,)), ((), ())), preferred_element_type=F32)
    for k in range(K):
        grad_store(0, k, down_grad[k * BLK : (k + 1) * BLK, :])

    def grad_copies(m, d, p):
        part = (gbuf.at[m, pl.ds(p * 4, 4)], grecv.at[m, d], gs_sem.at[m, d], gr_sem.at[m, d])
        scales = (gscale.at[m, p], gscale_in.at[m, d], gs_sem.at[2 + m, d], gr_sem.at[2 + m, d])
        return remote(*part, at_y(p)), remote(*scales, at_y(p))

    def grad_start(m):
        for d in range(1, NY):
            for copy in grad_copies(m, d, off(y, d, NY)):
                copy.start()

    grad_start(0)
    hidden_grad = jnp.dot(cot_in, down_tall, preferred_element_type=F32)
    pre_grad = (hidden_grad * squash * (1.0 + preact * (1.0 - squash))).astype(BF16)
    up_grad = lax.dot_general(pre_grad, a_in, (((0,), (0,)), ((), ())), preferred_element_type=F32)
    for k in range(K):
        grad_store(1, k, up_grad[:, k * BLK : (k + 1) * BLK])
    grad_start(1)

    for d in range(1, NS):
        p = off(s, -d, NS)
        remote(
            cbuf.at[p], rs_recv.at[p, pl.ds(0, K)], cs_sem.at[d], cr_sem.at[d], at_s(p)
        ).wait_recv()

    def gather_rows(r, carry):
        total = rs_recv[0, idx_s[0, 2, r]].astype(F32)
        for src in range(1, NS):
            total = total + rs_recv[src, idx_s[src, 2, r]].astype(F32)
        acc[pl.ds(pl.multiple_of(r * NZ, NZ), NZ), :] = total
        return carry

    lax.fori_loop(0, COLS, gather_rows, 0)
    for w in range(NZ):
        zsend[w] = acc[pl.ds(w, COLS, stride=NZ), :].astype(BF16)
    for d in (8, 7, 9, 6, 10, 5, 11, 4, 12, 3, 13, 2, 14, 1, 15):
        p = off(z, d, NZ)
        remote(zsend.at[p], zrecv.at[z], fs_sem.at[d], fr_sem.at[d], at_z(p)).start()
    zrecv[z] = zsend[z]

    for d in range(1, NY):
        p = off(y, -d, NY)
        remote(idx_y.at[0], idx_y.at[d], ys_sem.at[d], yr_sem.at[d], at_y(p)).wait_recv()
    count = idx_y[0, 3:4, :]
    for d in range(1, NY):
        count = count + idx_y[d, 3:4, :]
    per_token = 1.0 / count.astype(F32)

    def sum_copies(m, q, d, p):
        part = gsum.at[m, pl.ds(q * 4, 4)]
        scales = gsum_scale.at[m, q]
        return (
            remote(part, part, hs_sem.at[m, d], hr_sem.at[m, d], at_y(p)),
            remote(scales, scales, hs_sem.at[2 + m, d], hr_sem.at[2 + m, d], at_y(p)),
        )

    for m in range(2):
        for d in range(1, NY):
            for copy in grad_copies(m, d, off(y, -d, NY)):
                copy.wait_recv()
        for b in range(4):
            own = gbuf[m, y * 4 + b].astype(F32) * gscale[m, y, b : b + 1, :]
            for d in range(1, NY):
                own = own + grecv[m, d, b].astype(F32) * gscale_in[m, d, b : b + 1, :]
            code, scale = coded(own * per_token)
            gsum[m, y * 4 + b] = code
            gsum_scale[m, y, b : b + 1, :] = scale
        for d in range(1, NY):
            for copy in sum_copies(m, y, d, off(y, d, NY)):
                copy.start()

    for d in range(1, NZ):
        p = off(z, -d, NZ)
        remote(zsend.at[p], zrecv.at[p], fs_sem.at[d], fr_sem.at[d], at_z(p)).wait_recv()
    row = zrecv[0].astype(F32)
    for w in range(1, NZ):
        row = row + zrecv[w].astype(F32)
    layer_ref[...] = row * valid

    for m in range(2):
        for d in range(1, NY):
            p = off(y, -d, NY)
            for copy in sum_copies(m, p, d, p):
                copy.wait_recv()
        pltpu.make_async_copy(gsum.at[m], grad_hbm.at[m], o_sem.at[m]).start()
    pltpu.make_async_copy(gsum_scale, gscale_hbm, o_sem.at[2]).start()

    for m in range(2):
        for o in range(1, NZ):
            z_copy(m, z, off(z, 1, NZ), o).wait_send()
        for d in range(1, NS):
            remote(pack.at[m, d], picked.at[m, s], ps_sem.at[m, d], pr_sem.at[m, d], at_s(off(s, d, NS))).wait_send()
        for d in range(1, NY):
            p = off(y, d, NY)
            for copy in grad_copies(m, d, p) + sum_copies(m, y, d, p):
                copy.wait_send()
    for d in range(1, NS):
        p = off(s, d, NS)
        remote(idx_v.at[s], idx_v.at[s], is_sem.at[d], ir_sem.at[d], at_s(p)).wait_send()
        remote(cbuf.at[p], rs_recv.at[s, pl.ds(0, K)], cs_sem.at[d], cr_sem.at[d], at_s(p)).wait_send()
    for d in range(1, NY):
        remote(idx_y.at[0], idx_y.at[d], ys_sem.at[d], yr_sem.at[d], at_y(off(y, d, NY))).wait_send()
    for d in range(1, NZ):
        p = off(z, d, NZ)
        remote(zsend.at[p], zrecv.at[z], fs_sem.at[d], fr_sem.at[d], at_z(p)).wait_send()
    for m in range(2):
        pltpu.make_async_copy(gsum.at[m], grad_hbm.at[m], o_sem.at[m]).wait()
    pltpu.make_async_copy(gsum_scale, gscale_hbm, o_sem.at[2]).wait()


def exchange(tokens, cotangent, counts, up_cols, down_rows, up_blocks, down_blocks):
    vmem = pl.BlockSpec(memory_space=pltpu.VMEM)
    smem = pl.BlockSpec(memory_space=pltpu.SMEM)
    hbm = pl.BlockSpec(memory_space=pltpu.HBM)
    dma = pltpu.SemaphoreType.DMA
    return pl.pallas_call(
        exchange_kernel,
        out_shape=(
            jax.ShapeDtypeStruct((COLS, BLK), F32),
            jax.ShapeDtypeStruct((2, K, BLK, BLK), jnp.int16),
            jax.ShapeDtypeStruct((2, NY, 8, BLK), F32),
        ),
        in_specs=[hbm, hbm, smem, smem, smem, hbm, hbm],
        out_specs=(vmem, hbm, hbm),
        scratch_shapes=[
            pltpu.VMEM((1, D), BF16),
            pltpu.VMEM((1, D), BF16),
            pltpu.VMEM((K, BLK, BLK), BF16),
            pltpu.VMEM((K, BLK, BLK), BF16),
            pltpu.VMEM((NZ, 2 * COLS, BLK), BF16),
            pltpu.VMEM((2 * COLS, BLK), F32),
            pltpu.VMEM((2, COLS, NZ, BLK), F32),
            pltpu.VMEM((NS, 8, BLK), jnp.int32),
            pltpu.VMEM((NY, 8, BLK), jnp.int32),
            pltpu.SMEM((NS, 8, BLK), jnp.int32),
            pltpu.VMEM((2, NS, K, QROWS, BLK), BF16),
            pltpu.VMEM((2, NS, K, QROWS, BLK), BF16),
            pltpu.VMEM((NS, K, QROWS, BLK), BF16),
            pltpu.VMEM((NS, K + 1, QROWS, BLK), BF16),
            pltpu.VMEM((COLS * NZ, BLK), F32),
            pltpu.VMEM((NZ, COLS, BLK), BF16),
            pltpu.VMEM((NZ, COLS, BLK), BF16),
            pltpu.VMEM((2, K, BLK, BLK), jnp.int16),
            pltpu.VMEM((2, NY, 8, BLK), F32),
            pltpu.VMEM((2, NY, 4, BLK, BLK), jnp.int16),
            pltpu.VMEM((2, NY, 8, BLK), F32),
            pltpu.VMEM((2, K, BLK, BLK), jnp.int16),
            pltpu.VMEM((2, NY, 8, BLK), F32),
            dma((4,)),
            dma,
            dma((3,)),
            dma((2, NZ)),
            dma((2, NZ)),
            dma((NS,)),
            dma((NS,)),
            dma((NY,)),
            dma((NY,)),
            dma((2, NS)),
            dma((2, NS)),
            dma((NS,)),
            dma((NS,)),
            dma((NZ,)),
            dma((NZ,)),
            dma((4, NY)),
            dma((4, NY)),
            dma((4, NY)),
            dma((4, NY)),
        ],
        compiler_params=pltpu.CompilerParams(
            collective_id=1, has_side_effects=True, vmem_limit_bytes=60 << 20
        ),
        cost_estimate=pl.CostEstimate(flops=400_000_000, bytes_accessed=4 << 20, transcendentals=16384),
        name="exchange",
    )(tokens, cotangent, counts, up_cols, down_rows, up_blocks, down_blocks)


def adam_kernel(
    row_ref,
    grad_ref,
    gscale_ref,
    um_scale,
    us_scale,
    dm_scale,
    ds_scale,
    uw_ref,
    um_ref,
    us_ref,
    dw_ref,
    dm_ref,
    ds_ref,
    layer_ref,
    nuw_ref,
    num_ref,
    nums_ref,
    nus_ref,
    nuss_ref,
    ndw_ref,
    ndm_ref,
    ndms_ref,
    nds_ref,
    ndss_ref,
):
    step = pl.program_id(0)
    per_step = uw_ref.shape[0]

    @pl.when(step == 0)
    def _():
        for i in range(COLS):
            layer_ref[0:1, i * BLK : (i + 1) * BLK] = row_ref[i : i + 1, :].astype(BF16)
        for ref in (nums_ref, nuss_ref, ndms_ref, ndss_ref):
            ref[...] = jnp.zeros_like(ref)

    lane = lax.broadcasted_iota(jnp.int32, (8, K), 1)
    groups = BLK // QROWS
    sides = (
        (0, um_scale, us_scale, uw_ref, um_ref, us_ref, nuw_ref, num_ref, nums_ref, nus_ref, nuss_ref),
        (1, dm_scale, ds_scale, dw_ref, dm_ref, ds_ref, ndw_ref, ndm_ref, ndms_ref, nds_ref, ndss_ref),
    )
    for m, m_scale, s_scale, w_ref, m_ref, s_ref, nw_ref, nm_ref, nms_ref, ns_ref, nss_ref in sides:
        for b in range(per_step):
            block = step * per_step + b
            tops_m, tops_s = [], []
            g_scale = gscale_ref[1 - m, block // 4, pl.ds(block % 4, 1), :]
            for g in range(groups):
                rows = slice(g * QROWS, (g + 1) * QROWS)
                grad = grad_ref[1 - m, b, rows, :].astype(F32) * g_scale
                m_new = (beta_one * m_scale[g, block]) * m_ref[b, rows, :].astype(F32) + (
                    1.0 - beta_one
                ) * grad
                s_new = (beta_two * s_scale[g, block]) * s_ref[b, rows, :].astype(F32) + (
                    1.0 - beta_two
                ) * (grad * grad)
                direction = (m_new * (1.0 / bias_one)) / (jnp.sqrt(s_new * (1.0 / bias_two)) + adam_eps)
                w_old = w_ref[b, rows, :].astype(F32)
                nw_ref[b, rows, :] = (w_old - learn_rate * (direction + decay_rate * w_old)).astype(BF16)
                top_m = jnp.max(jnp.abs(m_new), axis=(0, 1), keepdims=True) + scale_eps
                top_s = jnp.max(s_new, axis=(0, 1), keepdims=True) + scale_eps
                nm_ref[b, rows, :] = (m_new * (1.0 / top_m)).astype(BF16)
                ns_ref[b, rows, :] = (s_new * (1.0 / top_s)).astype(BF16)
                tops_m.append(top_m)
                tops_s.append(top_s)
            nms_ref[...] = jnp.where(lane == block, jnp.concatenate(tops_m, axis=0), nms_ref[...])
            nss_ref[...] = jnp.where(lane == block, jnp.concatenate(tops_s, axis=0), nss_ref[...])


def adam(row, grads, gscales, up, down):
    steps = 8
    per = K // steps
    whole = lambda *shape: pl.BlockSpec(shape, lambda i: (0,) * len(shape))
    smem = pl.BlockSpec(memory_space=pltpu.SMEM)
    blocks = pl.BlockSpec((per, BLK, BLK), lambda i: (i, 0, 0))
    (uw, um, ums, us, uss) = up
    (dw, dm, dms, ds, dss) = down
    big = jax.ShapeDtypeStruct((K, BLK, BLK), BF16)
    small = jax.ShapeDtypeStruct((8, K), F32)
    out = pl.pallas_call(
        adam_kernel,
        grid=(steps,),
        in_specs=[
            whole(COLS, BLK),
            pl.BlockSpec((2, per, BLK, BLK), lambda i: (0, i, 0, 0)),
            whole(2, NY, 8, BLK),
            smem,
            smem,
            smem,
            smem,
        ]
        + [blocks] * 6,
        out_specs=[whole(1, D)] + [blocks, blocks, whole(8, K), blocks, whole(8, K)] * 2,
        out_shape=[jax.ShapeDtypeStruct((1, D), BF16)] + [big, big, small, big, small] * 2,
        compiler_params=pltpu.CompilerParams(vmem_limit_bytes=60 << 20),
        cost_estimate=pl.CostEstimate(flops=20_000_000, bytes_accessed=7 << 20, transcendentals=1_000_000),
        name="adam",
    )(row, grads, gscales, ums.T, uss.T, dms.T, dss.T, uw, um, us, dw, dm, ds)
    layer = out[0]
    nuw, num, nums, nus, nuss, ndw, ndm, ndms, nds, ndss = out[1:]
    return (layer, nuw, num, nums.T, nus, nuss.T, ndw, ndm, ndms.T, nds, ndss.T)


def per_device(
    tokens,
    counts,
    up_blocks,
    up_cols,
    down_blocks,
    down_rows,
    cotangent,
    up_moment,
    up_moment_scale,
    up_second,
    up_second_scale,
    down_moment,
    down_moment_scale,
    down_second,
    down_second_scale,
):
    row, grads, gscales = exchange(tokens, cotangent, counts, up_cols, down_rows, up_blocks, down_blocks)
    return adam(
        row,
        grads,
        gscales,
        (up_blocks, up_moment, up_moment_scale, up_second, up_second_scale),
        (down_blocks, down_moment, down_moment_scale, down_second, down_second_scale),
    )


def solution(mesh):
    spread = P(("dp", "mp"), None)
    blocks = P("mp", None, None)
    table = P("mp", None)
    side = (blocks, blocks, table, blocks, table)
    return jax.shard_map(
        per_device,
        mesh=mesh,
        in_specs=(spread, P("dp"), blocks, table, blocks, table, spread)
        + (blocks, table, blocks, table) * 2,
        out_specs=(spread,) + side + side,
        check_vma=False,
    )
```

```python
import functools

import jax
import jax.numpy as jnp
from jax import lax
from jax.experimental import pallas as pl
from jax.experimental.pallas import tpu as pltpu
from jax.sharding import PartitionSpec as P

D = 8192
BLK = 128
COLS = D // BLK
K = 16
NZ = 16
NS = 8
NY = 4
ROWS = 128
QROWS = 16
GROUPS = 8
CODE_TOP = 32767.0
Z_PEERS = (8, 4, -4, 2, -2, 1, -1)

beta_one = 0.9
beta_two = 0.99
learn_rate = 0.002
decay_rate = 0.1
adam_eps = 1e-08
scale_eps = 1e-06
bias_one = 1.0 - 0.9**10
bias_two = 1.0 - 0.99**10

MESH = pl.DeviceIdType.MESH
F32 = jnp.float32
BF16 = jnp.bfloat16


def exchange_kernel(*refs):
    (tokens_hbm, cot_hbm, counts_hbm, cols_hbm, rows_hbm) = refs[:5]
    states_hbm = (refs[5:8], refs[8:11])
    scales_hbm = refs[11:15]
    layer_hbm = refs[15]
    new_hbm = (refs[16:19], refs[19:22])
    new_scales_hbm = refs[22:26]
    (
        tokens_ref,
        cot_ref,
        counts_ref,
        cols_ref,
        rows_ref,
        layer_ref,
        states_v,
        scales_s,
        scales_v,
        zbuf,
        rowtmp,
        turned,
        idx_v,
        idx_y,
        idx_s,
        pack,
        picked,
        cbuf,
        rs_recv,
        acc,
        zsend,
        hub_in,
        hub_out,
        zrecv,
        gbuf,
        gscale,
        relay,
        rscale,
        grecv,
        gscale_in,
        gsum,
        gsum_scale,
        w_sem,
        i_sem,
        o_sem,
        zs_sem,
        zr_sem,
        is_sem,
        ir_sem,
        ys_sem,
        yr_sem,
        ps_sem,
        pr_sem,
        cs_sem,
        cr_sem,
        fs_sem,
        fr_sem,
        gs_sem,
        gr_sem,
    ) = refs[26:]
    y = lax.axis_index("dp")
    mp = lax.axis_index("mp")
    z = mp // NS
    s = mp % NS

    def at_z(p):
        return (y, p * NS + s)

    def at_s(p):
        return (y, z * NS + p)

    def at_y(p):
        return (p, mp)

    def off(a, d, n):
        return (a + (d % n)) % n

    def remote(src, dst, ssem, rsem, dev):
        return pltpu.make_async_remote_copy(
            src_ref=src, dst_ref=dst, send_sem=ssem, recv_sem=rsem, device_id=dev, device_id_type=MESH
        )

    barrier = pltpu.get_barrier_semaphore()
    for d in Z_PEERS:
        pl.semaphore_signal(barrier, inc=1, device_id=at_z(off(z, d, NZ)), device_id_type=MESH)
    for d in range(1, NS):
        pl.semaphore_signal(barrier, inc=1, device_id=at_s(off(s, d, NS)), device_id_type=MESH)
    for d in range(1, NY):
        pl.semaphore_signal(barrier, inc=1, device_id=at_y(off(y, d, NY)), device_id_type=MESH)

    loads = [
        pltpu.make_async_copy(src, dst, w_sem.at[i])
        for i, (src, dst) in enumerate(
            (
                (counts_hbm, counts_ref),
                (cols_hbm, cols_ref),
                (rows_hbm, rows_ref),
                (tokens_hbm, tokens_ref),
                (cot_hbm, cot_ref),
            )
        )
    ]
    state_loads = [
        [pltpu.make_async_copy(states_hbm[m][i], states_v.at[m, i], w_sem.at[5 + 3 * m + i]) for i in range(3)]
        for m in range(2)
    ]
    scale_loads = [pltpu.make_async_copy(scales_hbm[i], scales_s.at[i], w_sem.at[11 + i]) for i in range(4)]
    for copy in loads:
        copy.start()
    state_loads[1][0].start()
    state_loads[0][0].start()
    for copy in loads[:3]:
        copy.wait()

    valid = jnp.clip(counts_ref[0] - mp, 0, 1).astype(F32)

    sub = lax.broadcasted_iota(jnp.int32, (8, BLK), 0)
    lane = lax.broadcasted_iota(jnp.int32, (8, BLK), 1)
    tile = jnp.where(sub == 2, K, 0)
    for k in range(K):
        tile = jnp.where((sub == 0) & (lane == k), cols_ref[0, k], tile)
        tile = jnp.where((sub == 1) & (lane == k), rows_ref[0, k], tile)
        tile = jnp.where((sub == 2) & (lane == rows_ref[0, k]), k, tile)
    tile = jnp.where(sub == 3, counts_ref[0], tile)
    idx_v[s] = tile
    idx_y[0] = tile
    loads[3].wait()
    loads[4].wait()
    for m, ref in enumerate((tokens_ref, cot_ref)):
        for i in range(COLS):
            rowtmp[m * COLS + i : m * COLS + i + 1, :] = ref[0:1, i * BLK : (i + 1) * BLK].astype(F32)
    zbuf[z, 0:COLS, :] = rowtmp[0:COLS, :].astype(BF16)
    zbuf[z, COLS : 2 * COLS, :] = (rowtmp[COLS : 2 * COLS, :] * valid).astype(BF16)

    pl.semaphore_wait(barrier, len(Z_PEERS) + NS + NY - 2)

    def z_copy(m, w, p, o):
        part = zbuf.at[w, pl.ds(m * COLS, COLS), :]
        return remote(part, part, zs_sem.at[m, o], zr_sem.at[m, o], at_z(p))

    def z_start(m, h, e):
        z_copy(m, off(z, -h, NZ), off(z, e, NZ), (-h - e) % NZ).start()

    def z_wait(m, o):
        z_copy(m, off(z, o, NZ), off(z, 1, NZ), o).wait_recv()

    far = (8, 4, -4)
    near = ((2, 1, -1), (-2, 1, -1))

    for e in far:
        z_start(0, 0, e)
    for d in range(1, NS):
        remote(idx_v.at[s], idx_v.at[s], is_sem.at[d], ir_sem.at[d], at_s(off(s, d, NS))).start()
    for d in range(1, NY):
        remote(idx_y.at[0], idx_y.at[d], ys_sem.at[d], yr_sem.at[d], at_y(off(y, d, NY))).start()
    for e in near[0]:
        z_start(0, 0, e)
    for e in far:
        z_start(1, 0, e)
    for m in range(2):
        state_loads[m][1].start()
        state_loads[m][2].start()
    for copy in scale_loads:
        copy.start()
    for ref in (gscale, rscale, gsum_scale, scales_v):
        ref[...] = jnp.zeros_like(ref)
    for src in range(NS):
        rs_recv[src, K] = jnp.zeros((QROWS, BLK), BF16)

    for d in range(1, NS):
        p = off(s, -d, NS)
        remote(idx_v.at[p], idx_v.at[p], is_sem.at[d], ir_sem.at[d], at_s(p)).wait_recv()
    to_smem = pltpu.make_async_copy(idx_v, idx_s, i_sem)
    to_smem.start()

    for h in (4, -4, 8):
        z_wait(0, (-h) % NZ)
        for e in near[0]:
            z_start(0, h, e)
    for e in near[1]:
        z_start(1, 0, e)
    for h in (4, -4, 8):
        z_wait(1, (-h) % NZ)
        for e in near[1]:
            z_start(1, h, e)

    flat = turned.reshape(2, COLS * NZ, BLK)

    to_smem.wait()

    def pack_and_send(m):
        for o in range(1, NZ):
            if o % 4:
                z_wait(m, o)
        for w in range(NZ):
            flat[m, pl.ds(w, COLS, stride=NZ), :] = zbuf[w, m * COLS : (m + 1) * COLS, :].astype(F32)

        def one(i, carry):
            d = (s + i) % NS
            for k in range(K):
                pack[m, i, k] = turned[m, idx_s[d, m, k]].astype(BF16)
            remote(pack.at[m, i], picked.at[m, s], ps_sem.at[m, i], pr_sem.at[m, i], at_s(d)).start()
            return carry

        lax.fori_loop(1, NS, one, 0)
        for k in range(K):
            picked[m, s, k] = turned[m, idx_s[s, m, k]].astype(BF16)

    def wait_picked(m):
        for d in range(1, NS):
            p = off(s, -d, NS)
            remote(pack.at[m, d], picked.at[m, p], ps_sem.at[m, d], pr_sem.at[m, d], at_s(p)).wait_recv()
        return jnp.concatenate([picked[m, :, k].reshape(ROWS, BLK) for k in range(K)], axis=1)

    pack_and_send(0)
    pack_and_send(1)

    state_loads[1][0].wait()
    state_loads[0][0].wait()
    a_in = wait_picked(0)
    up_wide = jnp.concatenate([states_v[1, 0, k] for k in range(K)], axis=1)
    preact = lax.dot_general(a_in, up_wide, (((1,), (1,)), ((), ())), preferred_element_type=F32)
    squash = 1.0 / (1.0 + jnp.exp(-preact))
    hidden = (preact * squash).astype(BF16)
    down_tall = states_v[0, 0].reshape(K * BLK, BLK)
    contrib = lax.dot_general(hidden, down_tall, (((1,), (1,)), ((), ())), preferred_element_type=F32)
    for k in range(K):
        cbuf[:, k] = contrib[:, k * BLK : (k + 1) * BLK].astype(BF16).reshape(NS, QROWS, BLK)
    for d in range(1, NS):
        p = off(s, d, NS)
        remote(
            cbuf.at[p], rs_recv.at[s, pl.ds(0, K)], cs_sem.at[d], cr_sem.at[d], at_s(p)
        ).start()
    rs_recv[s, 0:K] = cbuf[s]

    def coded(grad):
        top = jnp.max(jnp.abs(grad), axis=0, keepdims=True)
        code = jnp.round(grad * (CODE_TOP / jnp.maximum(top, 1e-30)))
        return code.astype(jnp.int32).astype(jnp.int16), top * (1.0 / CODE_TOP)

    def grad_store(m, k, grad):
        code, scale = coded(grad)
        gbuf[m, k // 4, k // 2 % 2, k % 2] = code
        gscale[m, k // 4, k // 2 % 2, k % 2 : k % 2 + 1, :] = scale

    def pair(msg, m, buf, scl, at_src, to, to_scl, at_dst, p):
        return (
            remote(buf.at[at_src], to.at[at_dst], gs_sem.at[m, msg], gr_sem.at[m, msg], at_y(p)),
            remote(scl.at[at_src], to_scl.at[at_dst], gs_sem.at[m, 10 + msg], gr_sem.at[m, 10 + msg], at_y(p)),
        )

    left, right, across = off(y, -1, NY), off(y, 1, NY), off(y, 2, NY)

    def grad_msg(m, msg):
        raw, done = (m, gbuf, gscale), (m, gsum, gsum_scale)
        if msg == 0:
            return pair(msg, *raw, (m, across, 1), grecv, gscale_in, (m, 0), right)
        if msg == 1:
            return pair(msg, *raw, (m, across, 0), grecv, gscale_in, (m, 1), left)
        if msg == 2:
            return pair(msg, *raw, (m, right, 0), grecv, gscale_in, (m, 2), right)
        if msg == 3:
            return pair(msg, *raw, (m, left, 1), grecv, gscale_in, (m, 3), left)
        if msg == 4:
            return pair(msg, m, relay, rscale, (m, 1), grecv, gscale_in, (m, 4), right)
        if msg == 5:
            return pair(msg, m, relay, rscale, (m, 0), grecv, gscale_in, (m, 5), left)
        if msg == 6:
            return pair(msg, *done, (m, y), gsum, gsum_scale, (m, y), right)
        if msg == 7:
            return pair(msg, *done, (m, y), gsum, gsum_scale, (m, y), left)
        if msg == 8:
            return pair(msg, *done, (m, left, 1), gsum, gsum_scale, (m, left, 1), right)
        return pair(msg, *done, (m, right, 0), gsum, gsum_scale, (m, right, 0), left)

    def grad_send(m, *msgs):
        for msg in msgs:
            for copy in grad_msg(m, msg):
                copy.start()

    def grad_sent(m, *msgs):
        for msg in msgs:
            for copy in grad_msg(m, msg):
                copy.wait_send()

    def grad_wait(m, msg):
        for copy in grad_msg(m, msg):
            copy.wait_recv()

    def grad_back(m, msg, q):
        at = (m, q) if msg < 8 else (m, q, 9 - msg)
        for copy in pair(msg, m, gsum, gsum_scale, at, gsum, gsum_scale, at, left):
            copy.wait_recv()

    def value(buf, scl, at, b):
        return buf[(*at, b)].astype(F32) * scl[(*at, slice(b, b + 1), slice(None))]

    def pass_sum(m, msg, half, q, out):
        grad_wait(m, msg)
        for b in range(2):
            code, scale = coded(value(grecv, gscale_in, (m, msg), b) + value(gbuf, gscale, (m, q, half), b))
            relay[m, half, b] = code
            rscale[m, half, b : b + 1, :] = scale
        grad_send(m, out)

    def own_sum(m, half, msgs):
        for msg in msgs:
            grad_wait(m, msg)
        for b in range(2):
            total = value(gbuf, gscale, (m, y, half), b)
            for msg in msgs:
                total = total + value(grecv, gscale_in, (m, msg), b)
            code, scale = coded(total * per_token)
            gsum[m, y, half, b] = code
            gsum_scale[m, y, half, b : b + 1, :] = scale

    lane = lax.broadcasted_iota(jnp.int32, (8, K), 1)

    def adam(m, q):
        def block_step(i, carry):
            half, b = i // 2, i % 2
            block = q * 4 + i
            g_scale = gsum_scale[m, q, half, pl.ds(b, 1), :]
            moments, seconds = [], []
            for g in range(GROUPS):
                rows = slice(g * QROWS, (g + 1) * QROWS)
                grad = gsum[m, q, half, b, rows, :].astype(F32) * g_scale
                m_scale = beta_one * scales_s[2 * m, g, block]
                s_scale = beta_two * scales_s[2 * m + 1, g, block]
                m_new = m_scale * states_v[m, 1, block, rows, :].astype(F32) + (1.0 - beta_one) * grad
                s_new = s_scale * states_v[m, 2, block, rows, :].astype(F32) + (1.0 - beta_two) * (grad * grad)
                second = s_new * (1.0 / bias_two)
                root = second * lax.rsqrt(second) + adam_eps
                w_old = states_v[m, 0, block, rows, :].astype(F32)
                w_new = w_old * (1.0 - learn_rate * decay_rate) - (m_new * (learn_rate / bias_one)) * pl.reciprocal(
                    root, approx=True
                )
                states_v[m, 0, block, rows, :] = w_new.astype(BF16)
                moments.append(m_new)
                seconds.append(s_new)
            for j, values in ((0, moments), (1, seconds)):
                tops = jnp.concatenate([jnp.max(jnp.abs(v), axis=0, keepdims=True) for v in values], axis=0)
                top = jnp.max(tops, axis=1, keepdims=True) + scale_eps
                inverse = jnp.broadcast_to(1.0 / top, (8, BLK))
                for g in range(GROUPS):
                    rows = slice(g * QROWS, (g + 1) * QROWS)
                    states_v[m, 1 + j, block, rows, :] = (values[g] * inverse[g : g + 1, :]).astype(BF16)
                scales_v[2 * m + j] = jnp.where(lane == block, top, scales_v[2 * m + j])
            return carry

        lax.fori_loop(0, 4, block_step, 0)
        for i in range(3):
            out_copy(m, q, i).start()

    def out_copy(m, q, i):
        rows = pl.ds(q * 4, 4)
        return pltpu.make_async_copy(states_v.at[m, i, rows], new_hbm[m][i].at[rows], o_sem.at[m, i, q])

    cot_in = wait_picked(1)
    down_grad = lax.dot_general(cot_in, hidden, (((0,), (0,)), ((), ())), preferred_element_type=F32)
    for k in range(K):
        grad_store(0, k, down_grad[k * BLK : (k + 1) * BLK, :])

    grad_send(0, 0, 1, 2, 3)
    hidden_grad = jnp.dot(cot_in, down_tall, preferred_element_type=F32)
    pre_grad = (hidden_grad * squash * (1.0 + preact * (1.0 - squash))).astype(BF16)
    up_grad = lax.dot_general(pre_grad, a_in, (((0,), (0,)), ((), ())), preferred_element_type=F32)
    for k in range(K):
        grad_store(1, k, up_grad[:, k * BLK : (k + 1) * BLK])
    grad_send(1, 0, 1, 2, 3)

    for m in range(2):
        for o in range(1, NZ):
            z_copy(m, z, off(z, 1, NZ), o).wait_send()
        for d in range(1, NS):
            remote(pack.at[m, d], picked.at[m, s], ps_sem.at[m, d], pr_sem.at[m, d], at_s(off(s, d, NS))).wait_send()
    for d in range(1, NS):
        remote(idx_v.at[s], idx_v.at[s], is_sem.at[d], ir_sem.at[d], at_s(off(s, d, NS))).wait_send()
    for d in range(1, NY):
        remote(idx_y.at[0], idx_y.at[d], ys_sem.at[d], yr_sem.at[d], at_y(off(y, d, NY))).wait_send()
    for d in range(1, NY):
        p = off(y, -d, NY)
        remote(idx_y.at[0], idx_y.at[d], ys_sem.at[d], yr_sem.at[d], at_y(p)).wait_recv()
    count = idx_y[0, 3:4, :]
    for d in range(1, NY):
        count = count + idx_y[d, 3:4, :]
    per_token = 1.0 / count.astype(F32)

    pass_sum(0, 0, 1, right, 4)
    pass_sum(0, 1, 0, left, 5)

    for d in range(1, NS):
        p = off(s, -d, NS)
        remote(
            cbuf.at[p], rs_recv.at[p, pl.ds(0, K)], cs_sem.at[d], cr_sem.at[d], at_s(p)
        ).wait_recv()

    def gather_rows(r, carry):
        total = rs_recv[0, idx_s[0, 2, r]].astype(F32)
        for src in range(1, NS):
            total = total + rs_recv[src, idx_s[src, 2, r]].astype(F32)
        acc[pl.ds(pl.multiple_of(r * NZ, NZ), NZ), :] = total
        return carry

    lax.fori_loop(0, COLS, gather_rows, 0)
    for w in range(NZ):
        zsend[w % 4, w // 4] = acc[pl.ds(w, COLS, stride=NZ), :].astype(BF16)

    core = s % 2
    hubs = (off(z + 12 * core, 2, NZ), off(z, 1, NZ), off(z, -1, NZ))
    hub_from = (off(z + 4 * core, -2, NZ), off(z, -1, NZ), off(z, 1, NZ))

    def hub_copy(j, p):
        return remote(zsend.at[p % 4], hub_in.at[j], fs_sem.at[j], fr_sem.at[j], at_z(p))

    def row_copy(j, p):
        return remote(hub_out.at[p // 4], zrecv.at[j], fs_sem.at[4 + j], fr_sem.at[4 + j], at_z(p))

    for j in range(3):
        hub_copy(j, hubs[j]).start()

    pass_sum(1, 0, 1, right, 4)
    pass_sum(1, 1, 0, left, 5)
    own_sum(0, 0, (2, 5))
    own_sum(0, 1, (3, 4))
    grad_send(0, 6, 7)

    for j in range(3):
        hub_copy(j, hub_from[j]).wait_recv()
    for w in range(4):
        part = zsend[z % 4, w].astype(F32)
        for j in range(3):
            part = part + hub_in[j, w].astype(F32)
        hub_out[w] = part.astype(BF16)
    for j in (2, 1, 3):
        row_copy(j, off(z, 4 * j, NZ)).start()

    own_sum(1, 0, (2, 5))
    own_sum(1, 1, (3, 4))
    grad_send(1, 6, 7)
    for m in range(2):
        for i in (1, 2):
            state_loads[m][i].wait()
    for copy in scale_loads:
        copy.wait()
    adam(0, y)
    adam(1, y)
    grad_back(0, 6, left)
    grad_send(0, 8)
    grad_back(0, 7, right)
    grad_send(0, 9)

    grad_back(1, 6, left)
    grad_send(1, 8)
    grad_back(1, 7, right)
    grad_send(1, 9)
    adam(0, left)
    adam(0, right)
    for j in (1, 2, 3):
        row_copy(j, off(z, -4 * j, NZ)).wait_recv()
    row = hub_out[z // 4].astype(F32)
    for j in (1, 2, 3):
        row = row + zrecv[j].astype(F32)
    row = row * valid
    for i in range(COLS):
        layer_ref[0:1, i * BLK : (i + 1) * BLK] = row[i : i + 1, :].astype(BF16)
    layer_out = pltpu.make_async_copy(layer_ref, layer_hbm, w_sem.at[0])
    layer_out.start()
    for j in range(3):
        hub_copy(j, hubs[j]).wait_send()
    for j in (1, 2, 3):
        row_copy(j, off(z, 4 * j, NZ)).wait_send()
    for d in range(1, NS):
        p = off(s, d, NS)
        remote(cbuf.at[p], rs_recv.at[s, pl.ds(0, K)], cs_sem.at[d], cr_sem.at[d], at_s(p)).wait_send()
    for m in range(2):
        grad_sent(m, 0, 1, 2, 3, 4, 5)
    adam(1, left)
    adam(1, right)
    for m in range(2):
        grad_back(m, 8, across)
        grad_back(m, 9, across)
        adam(m, across)
    scale_out = [pltpu.make_async_copy(scales_v.at[i], new_scales_hbm[i], w_sem.at[1 + i]) for i in range(4)]
    for copy in scale_out:
        copy.start()
    for m in range(2):
        grad_sent(m, 6, 7, 8, 9)
    layer_out.wait()
    for m in range(2):
        for q in range(NY):
            for i in range(3):
                out_copy(m, q, i).wait()
    for copy in scale_out:
        copy.wait()


def deliver_kernel(*refs):
    n = 11
    held, in_sem, out_sem = refs[2 * n : 3 * n], refs[3 * n], refs[3 * n + 1]
    parts = []
    for i in range(n):
        if len(refs[i].shape) == 3:
            parts += [(i, pl.ds(0, K // 2)), (i, pl.ds(K // 2, K // 2))]
        else:
            parts.append((i, pl.ds(0, refs[i].shape[0])))
    loads = [pltpu.make_async_copy(refs[i].at[at], held[i].at[at], in_sem.at[j]) for j, (i, at) in enumerate(parts)]
    stores = [
        pltpu.make_async_copy(held[i].at[at], refs[n + i].at[at], out_sem.at[j]) for j, (i, at) in enumerate(parts)
    ]
    for load in loads:
        load.start()
    for load, store in zip(loads, stores):
        load.wait()
        store.start()
    for store in stores:
        store.wait()


def exchange(tokens, cotangent, counts, up_cols, down_rows, up, down):
    hbm = pl.BlockSpec(memory_space=pltpu.HBM)
    free = pl.BlockSpec(memory_space=pl.ANY)
    dma = pltpu.SemaphoreType.DMA
    (uw, um, ums, us, uss) = up
    (dw, dm, dms, ds, dss) = down
    big = jax.ShapeDtypeStruct((K, BLK, BLK), BF16)
    small = jax.ShapeDtypeStruct((GROUPS, K), F32)
    shapes = (jax.ShapeDtypeStruct((1, D), BF16),) + (big,) * 6 + (small,) * 4
    results = pl.pallas_call(
        exchange_kernel,
        out_shape=shapes,
        in_specs=[hbm] * 15,
        out_specs=(free,) * 11,
        scratch_shapes=[
            pltpu.VMEM((1, D), BF16),
            pltpu.VMEM((1, D), BF16),
            pltpu.SMEM((1,), jnp.int32),
            pltpu.SMEM((1, K), jnp.int32),
            pltpu.SMEM((1, K), jnp.int32),
            pltpu.VMEM((1, D), BF16),
            pltpu.VMEM((2, 3, K, BLK, BLK), BF16),
            pltpu.SMEM((4, GROUPS, K), F32),
            pltpu.VMEM((4, GROUPS, K), F32),
            pltpu.VMEM((NZ, 2 * COLS, BLK), BF16),
            pltpu.VMEM((2 * COLS, BLK), F32),
            pltpu.VMEM((2, COLS, NZ, BLK), F32),
            pltpu.VMEM((NS, 8, BLK), jnp.int32),
            pltpu.VMEM((NY, 8, BLK), jnp.int32),
            pltpu.SMEM((NS, 8, BLK), jnp.int32),
            pltpu.VMEM((2, NS, K, QROWS, BLK), BF16),
            pltpu.VMEM((2, NS, K, QROWS, BLK), BF16),
            pltpu.VMEM((NS, K, QROWS, BLK), BF16),
            pltpu.VMEM((NS, K + 1, QROWS, BLK), BF16),
            pltpu.VMEM((COLS * NZ, BLK), F32),
            pltpu.VMEM((4, 4, COLS, BLK), BF16),
            pltpu.VMEM((3, 4, COLS, BLK), BF16),
            pltpu.VMEM((4, COLS, BLK), BF16),
            pltpu.VMEM((4, COLS, BLK), BF16),
            pltpu.VMEM((2, NY, 2, 2, BLK, BLK), jnp.int16),
            pltpu.VMEM((2, NY, 2, 8, BLK), F32),
            pltpu.VMEM((2, 2, 2, BLK, BLK), jnp.int16),
            pltpu.VMEM((2, 2, 8, BLK), F32),
            pltpu.VMEM((2, 6, 2, BLK, BLK), jnp.int16),
            pltpu.VMEM((2, 6, 8, BLK), F32),
            pltpu.VMEM((2, NY, 2, 2, BLK, BLK), jnp.int16),
            pltpu.VMEM((2, NY, 2, 8, BLK), F32),
            dma((15,)),
            dma,
            dma((2, 3, NY)),
            dma((2, NZ)),
            dma((2, NZ)),
            dma((NS,)),
            dma((NS,)),
            dma((NY,)),
            dma((NY,)),
            dma((2, NS)),
            dma((2, NS)),
            dma((NS,)),
            dma((NS,)),
            dma((8,)),
            dma((8,)),
            dma((2, 20)),
            dma((2, 20)),
        ],
        compiler_params=pltpu.CompilerParams(
            collective_id=1, has_side_effects=True, vmem_limit_bytes=60 << 20
        ),
        cost_estimate=pl.CostEstimate(flops=400_000_000, bytes_accessed=8 << 20, transcendentals=1_000_000),
        name="exchange",
    )(
        tokens,
        cotangent,
        counts,
        up_cols,
        down_rows,
        dw,
        dm,
        ds,
        uw,
        um,
        us,
        dms.T,
        dss.T,
        ums.T,
        uss.T,
    )
    results = pl.pallas_call(
        deliver_kernel,
        out_shape=shapes,
        in_specs=[free] * 11,
        out_specs=(hbm,) * 11,
        scratch_shapes=[pltpu.VMEM(a.shape, a.dtype) for a in shapes] + [dma((17,)), dma((17,))],
        compiler_params=pltpu.CompilerParams(vmem_limit_bytes=60 << 20),
        name="deliver",
    )(*results)
    (layer, ndw, ndm, nds, nuw, num, nus, ndms, ndss, nums, nuss) = results
    return (layer, nuw, num, nums.T, nus, nuss.T, ndw, ndm, ndms.T, nds, ndss.T)


def per_device(
    tokens,
    counts,
    up_blocks,
    up_cols,
    down_blocks,
    down_rows,
    cotangent,
    up_moment,
    up_moment_scale,
    up_second,
    up_second_scale,
    down_moment,
    down_moment_scale,
    down_second,
    down_second_scale,
):
    return exchange(
        tokens,
        cotangent,
        counts,
        up_cols,
        down_rows,
        (up_blocks, up_moment, up_moment_scale, up_second, up_second_scale),
        (down_blocks, down_moment, down_moment_scale, down_second, down_second_scale),
    )


def solution(mesh):
    spread = P(("dp", "mp"), None)
    blocks = P("mp", None, None)
    table = P("mp", None)
    side = (blocks, blocks, table, blocks, table)
    return jax.shard_map(
        per_device,
        mesh=mesh,
        in_specs=(spread, P("dp"), blocks, table, blocks, table, spread)
        + (blocks, table, blocks, table) * 2,
        out_specs=(spread,) + side + side,
        check_vma=False,
    )
```

```python
import functools

import jax
import jax.numpy as jnp
from jax import lax
from jax.experimental import pallas as pl
from jax.experimental.pallas import tpu as pltpu
from jax.sharding import PartitionSpec as P

D = 8192
BLK = 128
COLS = D // BLK
K = 16
NZ = 16
NS = 8
NY = 4
ROWS = 128
QROWS = 16
GROUPS = 8
CODE_TOP = 32767.0
Z_PEERS = (8, 4, -4, 2, -2, 1, -1)

beta_one = 0.9
beta_two = 0.99
learn_rate = 0.002
decay_rate = 0.1
adam_eps = 1e-08
scale_eps = 1e-06
bias_one = 1.0 - 0.9**10
bias_two = 1.0 - 0.99**10

MESH = pl.DeviceIdType.MESH
F32 = jnp.float32
BF16 = jnp.bfloat16


def exchange_kernel(*refs):
    (tokens_hbm, cot_hbm, counts_hbm, cols_hbm, rows_hbm) = refs[:5]
    states_hbm = (refs[5:8], refs[8:11])
    scales_hbm = refs[11:15]
    layer_hbm = refs[15]
    new_hbm = (refs[16:19], refs[19:22])
    new_scales_hbm = refs[22:26]
    (
        tokens_ref,
        cot_ref,
        counts_ref,
        cols_ref,
        rows_ref,
        layer_ref,
        states_v,
        scales_s,
        scales_v,
        zbuf,
        rowtmp,
        turned,
        idx_v,
        idx_y,
        idx_s,
        pack,
        picked,
        cbuf,
        rs_recv,
        acc,
        zsend,
        hub_in,
        hub_out,
        zrecv,
        ypick,
        yact,
        gsum,
        gsum_scale,
        w_sem,
        i_sem,
        o_sem,
        zr_sem,
        s_sem,
        r_sem,
        gr_sem,
    ) = refs[26:]
    y = lax.axis_index("dp")
    mp = lax.axis_index("mp")
    z = mp // NS
    s = mp % NS

    def at_z(p):
        return (y, p * NS + s)

    def at_s(p):
        return (y, z * NS + p)

    def at_y(p):
        return (p, mp)

    def off(a, d, n):
        return (a + (d % n)) % n

    def remote(src, dst, ssem, rsem, dev):
        return pltpu.make_async_remote_copy(
            src_ref=src, dst_ref=dst, send_sem=ssem, recv_sem=rsem, device_id=dev, device_id_type=MESH
        )

    def arrived(part, sem):
        remote(part, part, sem, sem, at_y(off(y, 1, NY))).wait_recv()

    def left_here(part, sem):
        remote(part, part, sem, sem, at_y(off(y, 1, NY))).wait_send()

    barrier = pltpu.get_barrier_semaphore()
    for d in Z_PEERS:
        pl.semaphore_signal(barrier, inc=1, device_id=at_z(off(z, d, NZ)), device_id_type=MESH)
    for d in range(1, NS):
        pl.semaphore_signal(barrier, inc=1, device_id=at_s(off(s, d, NS)), device_id_type=MESH)
    for d in range(1, NY):
        pl.semaphore_signal(barrier, inc=1, device_id=at_y(off(y, d, NY)), device_id_type=MESH)

    loads = [
        pltpu.make_async_copy(src, dst, w_sem.at[i])
        for i, (src, dst) in enumerate(
            (
                (counts_hbm, counts_ref),
                (cols_hbm, cols_ref),
                (rows_hbm, rows_ref),
                (tokens_hbm, tokens_ref),
                (cot_hbm, cot_ref),
            )
        )
    ]
    state_loads = [
        [pltpu.make_async_copy(states_hbm[m][i], states_v.at[m, i], w_sem.at[5 + 2 * m + (i > 0)]) for i in range(3)]
        for m in range(2)
    ]
    scale_loads = [pltpu.make_async_copy(scales_hbm[i], scales_s.at[i], w_sem.at[9]) for i in range(4)]
    for copy in loads:
        copy.start()
    state_loads[1][0].start()
    state_loads[0][0].start()
    for copy in loads[:3]:
        copy.wait()

    valid = jnp.clip(counts_ref[0] - mp, 0, 1).astype(F32)

    sub = lax.broadcasted_iota(jnp.int32, (8, BLK), 0)
    lane = lax.broadcasted_iota(jnp.int32, (8, BLK), 1)
    tile = jnp.where(sub == 2, K, 0)
    for k in range(K):
        tile = jnp.where((sub == 0) & (lane == k), cols_ref[0, k], tile)
        tile = jnp.where((sub == 1) & (lane == k), rows_ref[0, k], tile)
        tile = jnp.where((sub == 2) & (lane == rows_ref[0, k]), k, tile)
    tile = jnp.where(sub == 3, counts_ref[0], tile)
    idx_v[s] = tile
    idx_y[0] = tile
    loads[3].wait()
    loads[4].wait()
    for m, ref in enumerate((tokens_ref, cot_ref)):
        for i in range(COLS):
            rowtmp[m * COLS + i : m * COLS + i + 1, :] = ref[0:1, i * BLK : (i + 1) * BLK].astype(F32)
    zbuf[z, 0:COLS, :] = rowtmp[0:COLS, :].astype(BF16)
    zbuf[z, COLS : 2 * COLS, :] = (rowtmp[COLS : 2 * COLS, :] * valid).astype(BF16)

    pl.semaphore_wait(barrier, len(Z_PEERS) + NS + NY - 2)

    def z_copy(m, w, p, o):
        part = zbuf.at[w, pl.ds(m * COLS, COLS), :]
        return remote(part, part, s_sem.at[0], zr_sem.at[m, o // 4 if o % 4 == 0 else 0], at_z(p))

    def z_start(m, h, e):
        z_copy(m, off(z, -h, NZ), off(z, e, NZ), (-h - e) % NZ).start()

    def z_wait(m, o):
        z_copy(m, off(z, o, NZ), off(z, 1, NZ), o).wait_recv()

    far = (8, 4, -4)
    near = ((2, 1, -1), (-2, 1, -1))

    for e in far:
        z_start(0, 0, e)
    for d in range(1, NS):
        remote(idx_v.at[s], idx_v.at[s], s_sem.at[1], r_sem.at[0], at_s(off(s, d, NS))).start()
    for d in range(1, NY):
        remote(idx_y.at[0], idx_y.at[d], s_sem.at[2], r_sem.at[1], at_y(off(y, d, NY))).start()
    for e in near[0]:
        z_start(0, 0, e)
    for e in far:
        z_start(1, 0, e)
    for m in range(2):
        state_loads[m][1].start()
        state_loads[m][2].start()
    for copy in scale_loads:
        copy.start()
    for ref in (gsum_scale, scales_v):
        ref[...] = jnp.zeros_like(ref)
    for src in range(NS):
        rs_recv[src, K] = jnp.zeros((QROWS, BLK), BF16)

    arrived(idx_v.at[pl.ds(0, NS - 1)], r_sem.at[0])
    to_smem = pltpu.make_async_copy(idx_v, idx_s, i_sem)
    to_smem.start()

    for h in (4, -4, 8):
        z_wait(0, (-h) % NZ)
        for e in near[0]:
            z_start(0, h, e)
    for e in near[1]:
        z_start(1, 0, e)
    for h in (4, -4, 8):
        z_wait(1, (-h) % NZ)
        for e in near[1]:
            z_start(1, h, e)

    flat = turned.reshape(2, COLS * NZ, BLK)

    to_smem.wait()

    def pack_and_send(m):
        arrived(zbuf.at[pl.ds(0, 6)], zr_sem.at[m, 0])
        for w in range(NZ):
            flat[m, pl.ds(w, COLS, stride=NZ), :] = zbuf[w, m * COLS : (m + 1) * COLS, :].astype(F32)

        def one(i, carry):
            d = (s + i) % NS
            for k in range(K):
                pack[m, i, k] = turned[m, idx_s[d, m, k]].astype(BF16)
            remote(pack.at[m, i], picked.at[m, s], s_sem.at[3], r_sem.at[2 + m], at_s(d)).start()
            return carry

        lax.fori_loop(1, NS, one, 0)
        for k in range(K):
            picked[m, s, k] = turned[m, idx_s[s, m, k]].astype(BF16)

    def wait_picked(m):
        arrived(picked.at[m, pl.ds(0, NS - 1)], r_sem.at[2 + m])
        return jnp.concatenate([picked[m, :, k].reshape(ROWS, BLK) for k in range(K)], axis=1)

    def y_copy(kind, d, p):
        if kind < 2:
            src, dst = picked.at[kind, :, pl.ds(p * 4, 4)], ypick.at[kind, d]
        else:
            src, dst = yact.at[kind - 2, 0], yact.at[kind - 2, d]
        return remote(src, dst, s_sem.at[7 + kind // 2], r_sem.at[7 + kind], at_y(p))

    def y_send(kind):
        for d in range(1, NY):
            y_copy(kind, d, off(y, d, NY)).start()

    pack_and_send(0)
    pack_and_send(1)

    state_loads[1][0].wait()
    state_loads[0][0].wait()
    a_in = wait_picked(0)
    y_send(0)
    up_wide = jnp.concatenate([states_v[1, 0, k] for k in range(K)], axis=1)
    preact = lax.dot_general(a_in, up_wide, (((1,), (1,)), ((), ())), preferred_element_type=F32)
    squash = 1.0 / (1.0 + jnp.exp(-preact))
    hidden = (preact * squash).astype(BF16)
    yact[0, 0] = hidden
    y_send(2)
    down_tall = states_v[0, 0].reshape(K * BLK, BLK)
    contrib = lax.dot_general(hidden, down_tall, (((1,), (1,)), ((), ())), preferred_element_type=F32)
    for k in range(K):
        cbuf[:, k] = contrib[:, k * BLK : (k + 1) * BLK].astype(BF16).reshape(NS, QROWS, BLK)
    for d in range(1, NS):
        p = off(s, d, NS)
        remote(
            cbuf.at[p], rs_recv.at[s, pl.ds(0, K)], s_sem.at[4], r_sem.at[4], at_s(p)
        ).start()
    rs_recv[s, 0:K] = cbuf[s]

    def coded(grad):
        top = jnp.max(jnp.abs(grad), axis=0, keepdims=True)
        code = jnp.round(grad * (CODE_TOP / jnp.maximum(top, 1e-30)))
        return code.astype(jnp.int32).astype(jnp.int16), top * (1.0 / CODE_TOP)

    left, right, across = off(y, -1, NY), off(y, 1, NY), off(y, 2, NY)

    def grad_msg(m, msg, at, p):
        part, scales = gsum.at[at], gsum_scale.at[at]
        return (
            remote(part, part, s_sem.at[9], gr_sem.at[m, msg], at_y(p)),
            remote(scales, scales, s_sem.at[10], gr_sem.at[m, 4 + msg], at_y(p)),
        )

    def grad_out(m, msg):
        at = ((m, y), (m, y), (m, left, 1), (m, right, 0))[msg]
        return grad_msg(m, msg, at, (right, left)[msg % 2])

    def grad_send(m, *msgs):
        for msg in msgs:
            for copy in grad_out(m, msg):
                copy.start()

    def grad_back(m, msg):
        at = ((m, left), (m, right), (m, across, 1), (m, across, 0))[msg]
        for copy in grad_msg(m, msg, at, left):
            copy.wait_recv()

    def own_grad(m):
        arrived(yact.at[m, pl.ds(0, NY - 1)], r_sem.at[9 + m])
        arrived(ypick.at[1 - m, pl.ds(0, NY - 1)], r_sem.at[8 - m])
        total = None
        for d in range(NY):
            if d:
                wide = jnp.concatenate([ypick[1 - m, d, :, k].reshape(ROWS, BLK) for k in range(4)], axis=1)
            else:
                wide = jnp.concatenate([picked[1 - m, :, y * 4 + k].reshape(ROWS, BLK) for k in range(4)], axis=1)
            narrow = yact[m, d]
            pair = (narrow, wide) if m else (wide, narrow)
            part = lax.dot_general(*pair, (((0,), (0,)), ((), ())), preferred_element_type=F32)
            total = part if total is None else total + part
        for k in range(4):
            cut = slice(k * BLK, (k + 1) * BLK)
            code, scale = coded((total[:, cut] if m else total[cut, :]) * per_token)
            gsum[m, y, k // 2, k % 2] = code
            gsum_scale[m, y, k // 2, k % 2 : k % 2 + 1, :] = scale

    lane = lax.broadcasted_iota(jnp.int32, (8, K), 1)

    def adam(m, q):
        def block_step(i, carry):
            half, b = i // 2, i % 2
            block = q * 4 + i
            g_scale = gsum_scale[m, q, half, pl.ds(b, 1), :]
            moments, seconds = [], []
            for g in range(GROUPS):
                rows = slice(g * QROWS, (g + 1) * QROWS)
                grad = gsum[m, q, half, b, rows, :].astype(F32) * g_scale
                m_scale = beta_one * scales_s[2 * m, g, block]
                s_scale = beta_two * scales_s[2 * m + 1, g, block]
                m_new = m_scale * states_v[m, 1, block, rows, :].astype(F32) + (1.0 - beta_one) * grad
                s_new = s_scale * states_v[m, 2, block, rows, :].astype(F32) + (1.0 - beta_two) * (grad * grad)
                second = s_new * (1.0 / bias_two)
                root = second * lax.rsqrt(second) + adam_eps
                w_old = states_v[m, 0, block, rows, :].astype(F32)
                w_new = w_old * (1.0 - learn_rate * decay_rate) - (m_new * (learn_rate / bias_one)) * pl.reciprocal(
                    root, approx=True
                )
                states_v[m, 0, block, rows, :] = w_new.astype(BF16)
                moments.append(m_new)
                seconds.append(s_new)
            for j, values in ((0, moments), (1, seconds)):
                tops = jnp.concatenate([jnp.max(jnp.abs(v), axis=0, keepdims=True) for v in values], axis=0)
                top = jnp.max(tops, axis=1, keepdims=True) + scale_eps
                inverse = jnp.broadcast_to(1.0 / top, (8, BLK))
                for g in range(GROUPS):
                    rows = slice(g * QROWS, (g + 1) * QROWS)
                    states_v[m, 1 + j, block, rows, :] = (values[g] * inverse[g : g + 1, :]).astype(BF16)
                scales_v[2 * m + j] = jnp.where(lane == block, top, scales_v[2 * m + j])
            return carry

        lax.fori_loop(0, 4, block_step, 0)
        for i in range(3):
            out_copy(m, q, i).start()

    def out_copy(m, q, i):
        rows = pl.ds(q * 4, 4)
        return pltpu.make_async_copy(states_v.at[m, i, rows], new_hbm[m][i].at[rows], o_sem)

    cot_in = wait_picked(1)
    hidden_grad = jnp.dot(cot_in, down_tall, preferred_element_type=F32)
    yact[1, 0] = (hidden_grad * squash * (1.0 + preact * (1.0 - squash))).astype(BF16)
    y_send(3)
    y_send(1)

    left_here(zbuf.at[pl.ds(0, NZ - 1)], s_sem.at[0])
    left_here(idx_v.at[pl.ds(0, NS - 1)], s_sem.at[1])
    left_here(idx_y.at[pl.ds(0, NY - 1)], s_sem.at[2])
    left_here(pack.at[:, pl.ds(1, NS - 1)], s_sem.at[3])
    arrived(idx_y.at[pl.ds(0, NY - 1)], r_sem.at[1])
    count = idx_y[0, 3:4, :]
    for d in range(1, NY):
        count = count + idx_y[d, 3:4, :]
    per_token = 1.0 / count.astype(F32)

    arrived(cbuf.at[pl.ds(0, NS - 1)], r_sem.at[4])

    def gather_rows(r, carry):
        total = rs_recv[0, idx_s[0, 2, r]].astype(F32)
        for src in range(1, NS):
            total = total + rs_recv[src, idx_s[src, 2, r]].astype(F32)
        acc[pl.ds(pl.multiple_of(r * NZ, NZ), NZ), :] = total
        return carry

    lax.fori_loop(0, COLS, gather_rows, 0)
    for w in range(NZ):
        zsend[w % 4, w // 4] = acc[pl.ds(w, COLS, stride=NZ), :].astype(BF16)

    core = s % 2
    hubs = (off(z + 12 * core, 2, NZ), off(z, 1, NZ), off(z, -1, NZ))

    def hub_copy(j, p):
        return remote(zsend.at[p % 4], hub_in.at[j], s_sem.at[5], r_sem.at[5], at_z(p))

    def row_copy(j, p):
        return remote(hub_out.at[p // 4], zrecv.at[j], s_sem.at[6], r_sem.at[6], at_z(p))

    for j in range(3):
        hub_copy(j, hubs[j]).start()

    own_grad(1)
    grad_send(1, 0, 1)
    own_grad(0)
    grad_send(0, 0, 1)

    arrived(hub_in, r_sem.at[5])
    for w in range(4):
        part = zsend[z % 4, w].astype(F32)
        for j in range(3):
            part = part + hub_in[j, w].astype(F32)
        hub_out[w] = part.astype(BF16)
    for j in (2, 1, 3):
        row_copy(j, off(z, 4 * j, NZ)).start()

    for m in range(2):
        both = states_v.at[m, pl.ds(1, 2)]
        pltpu.make_async_copy(both, both, w_sem.at[6 + 2 * m]).wait()
    pltpu.make_async_copy(scales_s, scales_s, w_sem.at[9]).wait()
    adam(1, y)
    grad_back(1, 0)
    grad_send(1, 2)
    grad_back(1, 1)
    grad_send(1, 3)
    adam(0, y)
    grad_back(0, 0)
    grad_send(0, 2)
    grad_back(0, 1)
    grad_send(0, 3)
    adam(1, left)
    adam(1, right)
    adam(0, left)
    adam(0, right)
    arrived(hub_out.at[pl.ds(0, 3)], r_sem.at[6])
    row = hub_out[z // 4].astype(F32)
    for j in (1, 2, 3):
        row = row + zrecv[j].astype(F32)
    row = row * valid
    for i in range(COLS):
        layer_ref[0:1, i * BLK : (i + 1) * BLK] = row[i : i + 1, :].astype(BF16)
    layer_out = pltpu.make_async_copy(layer_ref, layer_hbm, w_sem.at[0])
    layer_out.start()
    left_here(hub_in, s_sem.at[5])
    left_here(hub_out.at[pl.ds(0, 3)], s_sem.at[6])
    left_here(cbuf.at[pl.ds(0, NS - 1)], s_sem.at[4])
    left_here(ypick.at[:, pl.ds(0, NY - 1)], s_sem.at[7])
    left_here(yact.at[:, pl.ds(0, NY - 1)], s_sem.at[8])
    for m in (1, 0):
        grad_back(m, 2)
        grad_back(m, 3)
        adam(m, across)
    scale_out = [pltpu.make_async_copy(scales_v.at[i], new_scales_hbm[i], w_sem.at[1]) for i in range(4)]
    for copy in scale_out:
        copy.start()
    left_here(gsum.at[:, pl.ds(0, 3)], s_sem.at[9])
    left_here(gsum_scale.at[:, pl.ds(0, 3)], s_sem.at[10])
    layer_out.wait()
    pltpu.make_async_copy(states_v, states_v, o_sem).wait()
    pltpu.make_async_copy(scales_v, scales_v, w_sem.at[1]).wait()


def deliver_kernel(*refs):
    n = 11
    held, in_sem, out_sem = refs[2 * n : 3 * n], refs[3 * n], refs[3 * n + 1]
    parts = []
    for i in range(n):
        if len(refs[i].shape) == 3:
            parts += [(i, pl.ds(0, K // 2)), (i, pl.ds(K // 2, K // 2))]
        else:
            parts.append((i, pl.ds(0, refs[i].shape[0])))
    loads = [pltpu.make_async_copy(refs[i].at[at], held[i].at[at], in_sem.at[j]) for j, (i, at) in enumerate(parts)]
    stores = [
        pltpu.make_async_copy(held[i].at[at], refs[n + i].at[at], out_sem.at[i]) for i, at in parts
    ]
    for load in loads:
        load.start()
    for load, store in zip(loads, stores):
        load.wait()
        store.start()
    for i in range(n):
        pltpu.make_async_copy(held[i], refs[n + i], out_sem.at[i]).wait()


def exchange(tokens, cotangent, counts, up_cols, down_rows, up, down):
    hbm = pl.BlockSpec(memory_space=pltpu.HBM)
    free = pl.BlockSpec(memory_space=pl.ANY)
    dma = pltpu.SemaphoreType.DMA
    (uw, um, ums, us, uss) = up
    (dw, dm, dms, ds, dss) = down
    big = jax.ShapeDtypeStruct((K, BLK, BLK), BF16)
    small = jax.ShapeDtypeStruct((GROUPS, K), F32)
    shapes = (jax.ShapeDtypeStruct((1, D), BF16),) + (big,) * 6 + (small,) * 4
    results = pl.pallas_call(
        exchange_kernel,
        out_shape=shapes,
        in_specs=[hbm] * 15,
        out_specs=(free,) * 11,
        scratch_shapes=[
            pltpu.VMEM((1, D), BF16),
            pltpu.VMEM((1, D), BF16),
            pltpu.SMEM((1,), jnp.int32),
            pltpu.SMEM((1, K), jnp.int32),
            pltpu.SMEM((1, K), jnp.int32),
            pltpu.VMEM((1, D), BF16),
            pltpu.VMEM((2, 3, K, BLK, BLK), BF16),
            pltpu.SMEM((4, GROUPS, K), F32),
            pltpu.VMEM((4, GROUPS, K), F32),
            pltpu.VMEM((NZ, 2 * COLS, BLK), BF16),
            pltpu.VMEM((2 * COLS, BLK), F32),
            pltpu.VMEM((2, COLS, NZ, BLK), F32),
            pltpu.VMEM((NS, 8, BLK), jnp.int32),
            pltpu.VMEM((NY, 8, BLK), jnp.int32),
            pltpu.SMEM((NS, 8, BLK), jnp.int32),
            pltpu.VMEM((2, NS, K, QROWS, BLK), BF16),
            pltpu.VMEM((2, NS, K, QROWS, BLK), BF16),
            pltpu.VMEM((NS, K, QROWS, BLK), BF16),
            pltpu.VMEM((NS, K + 1, QROWS, BLK), BF16),
            pltpu.VMEM((COLS * NZ, BLK), F32),
            pltpu.VMEM((4, 4, COLS, BLK), BF16),
            pltpu.VMEM((3, 4, COLS, BLK), BF16),
            pltpu.VMEM((4, COLS, BLK), BF16),
            pltpu.VMEM((4, COLS, BLK), BF16),
            pltpu.VMEM((2, NY, NS, 4, QROWS, BLK), BF16),
            pltpu.VMEM((2, NY, ROWS, BLK), BF16),
            pltpu.VMEM((2, NY, 2, 2, BLK, BLK), jnp.int16),
            pltpu.VMEM((2, NY, 2, 8, BLK), F32),
            dma((10,)),
            dma,
            dma,
            dma((2, 4)),
            dma((11,)),
            dma((11,)),
            dma((2, 8)),
        ],
        compiler_params=pltpu.CompilerParams(
            collective_id=1, has_side_effects=True, vmem_limit_bytes=60 << 20
        ),
        cost_estimate=pl.CostEstimate(flops=400_000_000, bytes_accessed=8 << 20, transcendentals=1_000_000),
        name="exchange",
    )(
        tokens,
        cotangent,
        counts,
        up_cols,
        down_rows,
        dw,
        dm,
        ds,
        uw,
        um,
        us,
        dms.T,
        dss.T,
        ums.T,
        uss.T,
    )
    results = pl.pallas_call(
        deliver_kernel,
        out_shape=shapes,
        in_specs=[free] * 11,
        out_specs=(hbm,) * 11,
        scratch_shapes=[pltpu.VMEM(a.shape, a.dtype) for a in shapes] + [dma((17,)), dma((11,))],
        compiler_params=pltpu.CompilerParams(vmem_limit_bytes=60 << 20),
        name="deliver",
    )(*results)
    (layer, ndw, ndm, nds, nuw, num, nus, ndms, ndss, nums, nuss) = results
    return (layer, nuw, num, nums.T, nus, nuss.T, ndw, ndm, ndms.T, nds, ndss.T)


def per_device(
    tokens,
    counts,
    up_blocks,
    up_cols,
    down_blocks,
    down_rows,
    cotangent,
    up_moment,
    up_moment_scale,
    up_second,
    up_second_scale,
    down_moment,
    down_moment_scale,
    down_second,
    down_second_scale,
):
    return exchange(
        tokens,
        cotangent,
        counts,
        up_cols,
        down_rows,
        (up_blocks, up_moment, up_moment_scale, up_second, up_second_scale),
        (down_blocks, down_moment, down_moment_scale, down_second, down_second_scale),
    )


def solution(mesh):
    spread = P(("dp", "mp"), None)
    blocks = P("mp", None, None)
    table = P("mp", None)
    side = (blocks, blocks, table, blocks, table)
    return jax.shard_map(
        per_device,
        mesh=mesh,
        in_specs=(spread, P("dp"), blocks, table, blocks, table, spread)
        + (blocks, table, blocks, table) * 2,
        out_specs=(spread,) + side + side,
        check_vma=False,
    )
```

```python
import functools

import jax
import jax.numpy as jnp
from jax import lax
from jax.experimental import pallas as pl
from jax.experimental.pallas import tpu as pltpu
from jax.sharding import PartitionSpec as P

D = 8192
BLK = 128
COLS = D // BLK
K = 16
NZ = 16
NS = 8
NY = 4
ROWS = 128
QROWS = 16
GROUPS = 8
CODE_TOP = 32767.0
Z_PEERS = (8, 4, -4, 2, -2, 1, -1)

beta_one = 0.9
beta_two = 0.99
learn_rate = 0.002
decay_rate = 0.1
adam_eps = 1e-08
scale_eps = 1e-06
bias_one = 1.0 - 0.9**10
bias_two = 1.0 - 0.99**10

MESH = pl.DeviceIdType.MESH
F32 = jnp.float32
BF16 = jnp.bfloat16


def exchange_kernel(*refs):
    (tokens_hbm, cot_hbm, counts_hbm, cols_hbm, rows_hbm) = refs[:5]
    states_hbm = (refs[5:8], refs[8:11])
    scales_hbm = refs[11:15]
    layer_hbm = refs[15]
    new_hbm = (refs[16:19], refs[19:22])
    new_scales_hbm = refs[22:26]
    (
        tokens_ref,
        cot_ref,
        counts_ref,
        cols_ref,
        rows_ref,
        layer_ref,
        states_v,
        scales_s,
        scales_v,
        zbuf,
        rowtmp,
        turned,
        idx_v,
        idx_y,
        idx_s,
        pack,
        picked,
        cbuf,
        rs_recv,
        acc,
        zsend,
        hub_in,
        hub_out,
        zrecv,
        ypick,
        yact,
        gbuf,
        gscale,
        relay,
        rscale,
        grecv,
        gscale_in,
        gsum,
        gsum_scale,
        w_sem,
        i_sem,
        o_sem,
        zr_sem,
        s_sem,
        r_sem,
        gr_sem,
    ) = refs[26:]
    y = lax.axis_index("dp")
    mp = lax.axis_index("mp")
    z = mp // NS
    s = mp % NS

    def at_z(p):
        return (y, p * NS + s)

    def at_s(p):
        return (y, z * NS + p)

    def at_y(p):
        return (p, mp)

    def off(a, d, n):
        return (a + (d % n)) % n

    def remote(src, dst, ssem, rsem, dev):
        return pltpu.make_async_remote_copy(
            src_ref=src, dst_ref=dst, send_sem=ssem, recv_sem=rsem, device_id=dev, device_id_type=MESH
        )

    def arrived(part, sem):
        remote(part, part, sem, sem, at_y(off(y, 1, NY))).wait_recv()

    def left_here(part, sem):
        remote(part, part, sem, sem, at_y(off(y, 1, NY))).wait_send()

    barrier = pltpu.get_barrier_semaphore()
    for d in Z_PEERS:
        pl.semaphore_signal(barrier, inc=1, device_id=at_z(off(z, d, NZ)), device_id_type=MESH)
    for d in range(1, NS):
        pl.semaphore_signal(barrier, inc=1, device_id=at_s(off(s, d, NS)), device_id_type=MESH)
    for d in range(1, NY):
        pl.semaphore_signal(barrier, inc=1, device_id=at_y(off(y, d, NY)), device_id_type=MESH)

    loads = [
        pltpu.make_async_copy(src, dst, w_sem.at[i])
        for i, (src, dst) in enumerate(
            (
                (counts_hbm, counts_ref),
                (cols_hbm, cols_ref),
                (rows_hbm, rows_ref),
                (tokens_hbm, tokens_ref),
                (cot_hbm, cot_ref),
            )
        )
    ]
    state_loads = [
        [pltpu.make_async_copy(states_hbm[m][i], states_v.at[m, i], w_sem.at[5 + 2 * m + (i > 0)]) for i in range(3)]
        for m in range(2)
    ]
    scale_loads = [pltpu.make_async_copy(scales_hbm[i], scales_s.at[i], w_sem.at[9]) for i in range(4)]
    for copy in loads:
        copy.start()
    state_loads[1][0].start()
    state_loads[0][0].start()
    for copy in loads[:3]:
        copy.wait()

    valid = jnp.clip(counts_ref[0] - mp, 0, 1).astype(F32)

    sub = lax.broadcasted_iota(jnp.int32, (8, BLK), 0)
    lane = lax.broadcasted_iota(jnp.int32, (8, BLK), 1)
    tile = jnp.where(sub == 2, K, 0)
    for k in range(K):
        tile = jnp.where((sub == 0) & (lane == k), cols_ref[0, k], tile)
        tile = jnp.where((sub == 1) & (lane == k), rows_ref[0, k], tile)
        tile = jnp.where((sub == 2) & (lane == rows_ref[0, k]), k, tile)
    tile = jnp.where(sub == 3, counts_ref[0], tile)
    idx_v[s] = tile
    idx_y[0] = tile
    loads[3].wait()
    loads[4].wait()
    for m, ref in enumerate((tokens_ref, cot_ref)):
        for i in range(COLS):
            rowtmp[m * COLS + i : m * COLS + i + 1, :] = ref[0:1, i * BLK : (i + 1) * BLK].astype(F32)
    zbuf[z, 0:COLS, :] = rowtmp[0:COLS, :].astype(BF16)
    zbuf[z, COLS : 2 * COLS, :] = (rowtmp[COLS : 2 * COLS, :] * valid).astype(BF16)

    pl.semaphore_wait(barrier, len(Z_PEERS) + NS + NY - 2)

    def z_copy(m, w, p, o):
        part = zbuf.at[w, pl.ds(m * COLS, COLS), :]
        return remote(part, part, s_sem.at[0], zr_sem.at[m, o // 4 if o % 4 == 0 else 0], at_z(p))

    def z_start(m, h, e):
        z_copy(m, off(z, -h, NZ), off(z, e, NZ), (-h - e) % NZ).start()

    def z_wait(m, o):
        z_copy(m, off(z, o, NZ), off(z, 1, NZ), o).wait_recv()

    far = (8, 4, -4)
    near = ((2, 1, -1), (-2, 1, -1))

    for e in far:
        z_start(0, 0, e)
    for d in range(1, NS):
        remote(idx_v.at[s], idx_v.at[s], s_sem.at[1], r_sem.at[0], at_s(off(s, d, NS))).start()
    for d in range(1, NY):
        remote(idx_y.at[0], idx_y.at[d], s_sem.at[2], r_sem.at[1], at_y(off(y, d, NY))).start()
    for e in near[0]:
        z_start(0, 0, e)
    for e in far:
        z_start(1, 0, e)
    for m in range(2):
        state_loads[m][1].start()
        state_loads[m][2].start()
    for copy in scale_loads:
        copy.start()
    for ref in (gscale, rscale, gsum_scale, scales_v):
        ref[...] = jnp.zeros_like(ref)
    for src in range(NS):
        rs_recv[src, K] = jnp.zeros((QROWS, BLK), BF16)

    arrived(idx_v.at[pl.ds(0, NS - 1)], r_sem.at[0])
    to_smem = pltpu.make_async_copy(idx_v, idx_s, i_sem)
    to_smem.start()

    for h in (4, -4, 8):
        z_wait(0, (-h) % NZ)
        for e in near[0]:
            z_start(0, h, e)
    for e in near[1]:
        z_start(1, 0, e)
    for h in (4, -4, 8):
        z_wait(1, (-h) % NZ)
        for e in near[1]:
            z_start(1, h, e)

    flat = turned.reshape(2, COLS * NZ, BLK)

    to_smem.wait()

    def pack_and_send(m):
        arrived(zbuf.at[pl.ds(0, 6)], zr_sem.at[m, 0])
        for w in range(NZ):
            flat[m, pl.ds(w, COLS, stride=NZ), :] = zbuf[w, m * COLS : (m + 1) * COLS, :].astype(F32)

        def one(i, carry):
            d = (s + i) % NS
            for k in range(K):
                pack[m, i, k] = turned[m, idx_s[d, m, k]].astype(BF16)
            remote(pack.at[m, i], picked.at[m, s], s_sem.at[3], r_sem.at[2 + m], at_s(d)).start()
            return carry

        lax.fori_loop(1, NS, one, 0)
        for k in range(K):
            picked[m, s, k] = turned[m, idx_s[s, m, k]].astype(BF16)

    def wait_picked(m):
        arrived(picked.at[m, pl.ds(0, NS - 1)], r_sem.at[2 + m])
        return jnp.concatenate([picked[m, :, k].reshape(ROWS, BLK) for k in range(K)], axis=1)

    def y_copy(kind, d, p):
        if kind:
            src, dst = yact.at[0], yact.at[d]
        else:
            src, dst = picked.at[0, :, pl.ds(p * 4, 4)], ypick.at[d]
        return remote(src, dst, s_sem.at[7 + kind], r_sem.at[7 + kind], at_y(p))

    def y_send(kind):
        for d in range(1, NY):
            y_copy(kind, d, off(y, d, NY)).start()

    pack_and_send(0)
    pack_and_send(1)

    state_loads[1][0].wait()
    state_loads[0][0].wait()
    a_in = wait_picked(0)
    y_send(0)
    up_wide = jnp.concatenate([states_v[1, 0, k] for k in range(K)], axis=1)
    preact = lax.dot_general(a_in, up_wide, (((1,), (1,)), ((), ())), preferred_element_type=F32)
    squash = 1.0 / (1.0 + jnp.exp(-preact))
    hidden = (preact * squash).astype(BF16)
    down_tall = states_v[0, 0].reshape(K * BLK, BLK)
    contrib = lax.dot_general(hidden, down_tall, (((1,), (1,)), ((), ())), preferred_element_type=F32)
    for k in range(K):
        cbuf[:, k] = contrib[:, k * BLK : (k + 1) * BLK].astype(BF16).reshape(NS, QROWS, BLK)
    for d in range(1, NS):
        p = off(s, d, NS)
        remote(
            cbuf.at[p], rs_recv.at[s, pl.ds(0, K)], s_sem.at[4], r_sem.at[4], at_s(p)
        ).start()
    rs_recv[s, 0:K] = cbuf[s]

    def coded(grad):
        top = jnp.max(jnp.abs(grad), axis=0, keepdims=True)
        code = jnp.round(grad * (CODE_TOP / jnp.maximum(top, 1e-30)))
        return code.astype(jnp.int32).astype(jnp.int16), top * (1.0 / CODE_TOP)

    left, right, across = off(y, -1, NY), off(y, 1, NY), off(y, 2, NY)

    def grad_msg(m, msg, at, p):
        part, scales = gsum.at[at], gsum_scale.at[at]
        return (
            remote(part, part, s_sem.at[9], gr_sem.at[m, msg], at_y(p)),
            remote(scales, scales, s_sem.at[10], gr_sem.at[m, 4 + msg], at_y(p)),
        )

    def grad_out(m, msg):
        at = ((m, y), (m, y), (m, left, 1), (m, right, 0))[msg]
        return grad_msg(m, msg, at, (right, left)[msg % 2])

    def grad_send(m, *msgs):
        for msg in msgs:
            for copy in grad_out(m, msg):
                copy.start()

    def grad_back(m, msg):
        at = ((m, left), (m, right), (m, across, 1), (m, across, 0))[msg]
        for copy in grad_msg(m, msg, at, left):
            copy.wait_recv()

    def own_store(m, half, b, total):
        code, scale = coded(total * per_token)
        gsum[m, y, half, b] = code
        gsum_scale[m, y, half, b : b + 1, :] = scale

    def own_up():
        arrived(yact.at[pl.ds(0, NY - 1)], r_sem.at[8])
        arrived(ypick.at[pl.ds(0, NY - 1)], r_sem.at[7])
        total = None
        for d in range(NY):
            if d:
                wide = jnp.concatenate([ypick[d, :, k].reshape(ROWS, BLK) for k in range(4)], axis=1)
            else:
                wide = jnp.concatenate([picked[0, :, y * 4 + k].reshape(ROWS, BLK) for k in range(4)], axis=1)
            part = lax.dot_general(yact[d], wide, (((0,), (0,)), ((), ())), preferred_element_type=F32)
            total = part if total is None else total + part
        for k in range(4):
            own_store(1, k // 2, k % 2, total[:, k * BLK : (k + 1) * BLK])

    def ring(msg):
        if msg < 4:
            at = ((across, 1), (across, 0), (right, 0), (left, 1))[msg]
            src, scl = gbuf.at[at], gscale.at[at]
        else:
            src, scl = relay.at[5 - msg], rscale.at[5 - msg]
        to = at_y((right, left)[msg % 2])
        r = 11 if msg < 2 else 13
        return (
            remote(src, grecv.at[msg], s_sem.at[11], r_sem.at[r], to),
            remote(scl, gscale_in.at[msg], s_sem.at[12], r_sem.at[r + 1], to),
        )

    def ring_send(*msgs):
        for msg in msgs:
            for copy in ring(msg):
                copy.start()

    def own_value(q, half, b):
        return gbuf[q, half, b].astype(F32) * gscale[q, half, b : b + 1, :]

    def came(msg, b):
        return grecv[msg, b].astype(F32) * gscale_in[msg, b : b + 1, :]

    def ring_pass():
        arrived(grecv.at[pl.ds(0, 2)], r_sem.at[11])
        arrived(gscale_in.at[pl.ds(0, 2)], r_sem.at[12])
        for msg, q in ((0, right), (1, left)):
            for b in range(2):
                code, scale = coded(came(msg, b) + own_value(q, 1 - msg, b))
                relay[1 - msg, b] = code
                rscale[1 - msg, b : b + 1, :] = scale
        ring_send(4, 5)

    def own_down():
        arrived(grecv.at[pl.ds(2, 4)], r_sem.at[13])
        arrived(gscale_in.at[pl.ds(2, 4)], r_sem.at[14])
        for half in range(2):
            for b in range(2):
                own_store(0, half, b, own_value(y, half, b) + came(2 + half, b) + came(5 - half, b))

    lane = lax.broadcasted_iota(jnp.int32, (8, K), 1)

    def adam(m, q):
        def block_step(i, carry):
            half, b = i // 2, i % 2
            block = q * 4 + i
            g_scale = gsum_scale[m, q, half, pl.ds(b, 1), :]
            moments, seconds = [], []
            for g in range(GROUPS):
                rows = slice(g * QROWS, (g + 1) * QROWS)
                grad = gsum[m, q, half, b, rows, :].astype(F32) * g_scale
                m_scale = beta_one * scales_s[2 * m, g, block]
                s_scale = beta_two * scales_s[2 * m + 1, g, block]
                m_new = m_scale * states_v[m, 1, block, rows, :].astype(F32) + (1.0 - beta_one) * grad
                s_new = s_scale * states_v[m, 2, block, rows, :].astype(F32) + (1.0 - beta_two) * (grad * grad)
                second = s_new * (1.0 / bias_two)
                root = second * lax.rsqrt(second) + adam_eps
                w_old = states_v[m, 0, block, rows, :].astype(F32)
                w_new = w_old * (1.0 - learn_rate * decay_rate) - (m_new * (learn_rate / bias_one)) * pl.reciprocal(
                    root, approx=True
                )
                states_v[m, 0, block, rows, :] = w_new.astype(BF16)
                moments.append(m_new)
                seconds.append(s_new)
            for j, values in ((0, moments), (1, seconds)):
                tops = jnp.concatenate([jnp.max(jnp.abs(v), axis=0, keepdims=True) for v in values], axis=0)
                top = jnp.max(tops, axis=1, keepdims=True) + scale_eps
                inverse = jnp.broadcast_to(1.0 / top, (8, BLK))
                for g in range(GROUPS):
                    rows = slice(g * QROWS, (g + 1) * QROWS)
                    states_v[m, 1 + j, block, rows, :] = (values[g] * inverse[g : g + 1, :]).astype(BF16)
                scales_v[2 * m + j] = jnp.where(lane == block, top, scales_v[2 * m + j])
            return carry

        lax.fori_loop(0, 4, block_step, 0)
        for i in range(3):
            out_copy(m, q, i).start()

    def out_copy(m, q, i):
        rows = pl.ds(q * 4, 4)
        return pltpu.make_async_copy(states_v.at[m, i, rows], new_hbm[m][i].at[rows], o_sem)

    cot_in = wait_picked(1)
    down_grad = lax.dot_general(cot_in, hidden, (((0,), (0,)), ((), ())), preferred_element_type=F32)
    for k in range(K):
        code, scale = coded(down_grad[k * BLK : (k + 1) * BLK, :])
        gbuf[k // 4, k // 2 % 2, k % 2] = code
        gscale[k // 4, k // 2 % 2, k % 2 : k % 2 + 1, :] = scale
    ring_send(0, 1)
    hidden_grad = jnp.dot(cot_in, down_tall, preferred_element_type=F32)
    yact[0] = (hidden_grad * squash * (1.0 + preact * (1.0 - squash))).astype(BF16)
    y_send(1)
    ring_send(2, 3)

    left_here(zbuf.at[pl.ds(0, NZ - 1)], s_sem.at[0])
    left_here(idx_v.at[pl.ds(0, NS - 1)], s_sem.at[1])
    left_here(idx_y.at[pl.ds(0, NY - 1)], s_sem.at[2])
    left_here(pack.at[:, pl.ds(1, NS - 1)], s_sem.at[3])
    arrived(idx_y.at[pl.ds(0, NY - 1)], r_sem.at[1])
    count = idx_y[0, 3:4, :]
    for d in range(1, NY):
        count = count + idx_y[d, 3:4, :]
    per_token = 1.0 / count.astype(F32)

    ring_pass()

    arrived(cbuf.at[pl.ds(0, NS - 1)], r_sem.at[4])

    def gather_rows(r, carry):
        total = rs_recv[0, idx_s[0, 2, r]].astype(F32)
        for src in range(1, NS):
            total = total + rs_recv[src, idx_s[src, 2, r]].astype(F32)
        acc[pl.ds(pl.multiple_of(r * NZ, NZ), NZ), :] = total
        return carry

    lax.fori_loop(0, COLS, gather_rows, 0)
    for w in range(NZ):
        zsend[w % 4, w // 4] = acc[pl.ds(w, COLS, stride=NZ), :].astype(BF16)

    core = s % 2
    hubs = (off(z + 12 * core, 2, NZ), off(z, 1, NZ), off(z, -1, NZ))

    def hub_copy(j, p):
        return remote(zsend.at[p % 4], hub_in.at[j], s_sem.at[5], r_sem.at[5], at_z(p))

    def row_copy(j, p):
        return remote(hub_out.at[p // 4], zrecv.at[j], s_sem.at[6], r_sem.at[6], at_z(p))

    for j in range(3):
        hub_copy(j, hubs[j]).start()

    own_up()
    grad_send(1, 0, 1)
    own_down()
    grad_send(0, 0, 1)

    arrived(hub_in, r_sem.at[5])
    for w in range(4):
        part = zsend[z % 4, w].astype(F32)
        for j in range(3):
            part = part + hub_in[j, w].astype(F32)
        hub_out[w] = part.astype(BF16)
    for j in (2, 1, 3):
        row_copy(j, off(z, 4 * j, NZ)).start()

    for m in range(2):
        both = states_v.at[m, pl.ds(1, 2)]
        pltpu.make_async_copy(both, both, w_sem.at[6 + 2 * m]).wait()
    pltpu.make_async_copy(scales_s, scales_s, w_sem.at[9]).wait()
    adam(1, y)
    grad_back(1, 0)
    grad_send(1, 2)
    grad_back(1, 1)
    grad_send(1, 3)
    adam(0, y)
    grad_back(0, 0)
    grad_send(0, 2)
    grad_back(0, 1)
    grad_send(0, 3)
    adam(1, left)
    adam(1, right)
    adam(0, left)
    adam(0, right)
    arrived(hub_out.at[pl.ds(0, 3)], r_sem.at[6])
    row = hub_out[z // 4].astype(F32)
    for j in (1, 2, 3):
        row = row + zrecv[j].astype(F32)
    row = row * valid
    for i in range(COLS):
        layer_ref[0:1, i * BLK : (i + 1) * BLK] = row[i : i + 1, :].astype(BF16)
    layer_out = pltpu.make_async_copy(layer_ref, layer_hbm, w_sem.at[0])
    layer_out.start()
    left_here(hub_in, s_sem.at[5])
    left_here(hub_out.at[pl.ds(0, 3)], s_sem.at[6])
    left_here(cbuf.at[pl.ds(0, NS - 1)], s_sem.at[4])
    left_here(ypick.at[pl.ds(0, NY - 1)], s_sem.at[7])
    left_here(yact.at[pl.ds(0, NY - 1)], s_sem.at[8])
    left_here(grecv, s_sem.at[11])
    left_here(gscale_in, s_sem.at[12])
    for m in (1, 0):
        grad_back(m, 2)
        grad_back(m, 3)
        adam(m, across)
    scale_out = [pltpu.make_async_copy(scales_v.at[i], new_scales_hbm[i], w_sem.at[1]) for i in range(4)]
    for copy in scale_out:
        copy.start()
    left_here(gsum.at[:, pl.ds(0, 3)], s_sem.at[9])
    left_here(gsum_scale.at[:, pl.ds(0, 3)], s_sem.at[10])
    layer_out.wait()
    pltpu.make_async_copy(states_v, states_v, o_sem).wait()
    pltpu.make_async_copy(scales_v, scales_v, w_sem.at[1]).wait()


def deliver_kernel(*refs):
    n = 11
    held, in_sem, out_sem = refs[2 * n : 3 * n], refs[3 * n], refs[3 * n + 1]
    parts = []
    for i in range(n):
        if len(refs[i].shape) == 3:
            parts += [(i, pl.ds(0, K // 2)), (i, pl.ds(K // 2, K // 2))]
        else:
            parts.append((i, pl.ds(0, refs[i].shape[0])))
    loads = [pltpu.make_async_copy(refs[i].at[at], held[i].at[at], in_sem.at[j]) for j, (i, at) in enumerate(parts)]
    stores = [
        pltpu.make_async_copy(held[i].at[at], refs[n + i].at[at], out_sem.at[i]) for i, at in parts
    ]
    for load in loads:
        load.start()
    for load, store in zip(loads, stores):
        load.wait()
        store.start()
    for i in range(n):
        pltpu.make_async_copy(held[i], refs[n + i], out_sem.at[i]).wait()


def exchange(tokens, cotangent, counts, up_cols, down_rows, up, down):
    hbm = pl.BlockSpec(memory_space=pltpu.HBM)
    free = pl.BlockSpec(memory_space=pl.ANY)
    dma = pltpu.SemaphoreType.DMA
    (uw, um, ums, us, uss) = up
    (dw, dm, dms, ds, dss) = down
    big = jax.ShapeDtypeStruct((K, BLK, BLK), BF16)
    small = jax.ShapeDtypeStruct((GROUPS, K), F32)
    shapes = (jax.ShapeDtypeStruct((1, D), BF16),) + (big,) * 6 + (small,) * 4
    results = pl.pallas_call(
        exchange_kernel,
        out_shape=shapes,
        in_specs=[hbm] * 15,
        out_specs=(free,) * 11,
        scratch_shapes=[
            pltpu.VMEM((1, D), BF16),
            pltpu.VMEM((1, D), BF16),
            pltpu.SMEM((1,), jnp.int32),
            pltpu.SMEM((1, K), jnp.int32),
            pltpu.SMEM((1, K), jnp.int32),
            pltpu.VMEM((1, D), BF16),
            pltpu.VMEM((2, 3, K, BLK, BLK), BF16),
            pltpu.SMEM((4, GROUPS, K), F32),
            pltpu.VMEM((4, GROUPS, K), F32),
            pltpu.VMEM((NZ, 2 * COLS, BLK), BF16),
            pltpu.VMEM((2 * COLS, BLK), F32),
            pltpu.VMEM((2, COLS, NZ, BLK), F32),
            pltpu.VMEM((NS, 8, BLK), jnp.int32),
            pltpu.VMEM((NY, 8, BLK), jnp.int32),
            pltpu.SMEM((NS, 8, BLK), jnp.int32),
            pltpu.VMEM((2, NS, K, QROWS, BLK), BF16),
            pltpu.VMEM((2, NS, K, QROWS, BLK), BF16),
            pltpu.VMEM((NS, K, QROWS, BLK), BF16),
            pltpu.VMEM((NS, K + 1, QROWS, BLK), BF16),
            pltpu.VMEM((COLS * NZ, BLK), F32),
            pltpu.VMEM((4, 4, COLS, BLK), BF16),
            pltpu.VMEM((3, 4, COLS, BLK), BF16),
            pltpu.VMEM((4, COLS, BLK), BF16),
            pltpu.VMEM((4, COLS, BLK), BF16),
            pltpu.VMEM((NY, NS, 4, QROWS, BLK), BF16),
            pltpu.VMEM((NY, ROWS, BLK), BF16),
            pltpu.VMEM((NY, 2, 2, BLK, BLK), jnp.int16),
            pltpu.VMEM((NY, 2, 8, BLK), F32),
            pltpu.VMEM((2, 2, BLK, BLK), jnp.int16),
            pltpu.VMEM((2, 8, BLK), F32),
            pltpu.VMEM((6, 2, BLK, BLK), jnp.int16),
            pltpu.VMEM((6, 8, BLK), F32),
            pltpu.VMEM((2, NY, 2, 2, BLK, BLK), jnp.int16),
            pltpu.VMEM((2, NY, 2, 8, BLK), F32),
            dma((10,)),
            dma,
            dma,
            dma((2, 4)),
            dma((13,)),
            dma((15,)),
            dma((2, 8)),
        ],
        compiler_params=pltpu.CompilerParams(
            collective_id=1, has_side_effects=True, vmem_limit_bytes=60 << 20
        ),
        cost_estimate=pl.CostEstimate(flops=400_000_000, bytes_accessed=8 << 20, transcendentals=1_000_000),
        name="exchange",
    )(
        tokens,
        cotangent,
        counts,
        up_cols,
        down_rows,
        dw,
        dm,
        ds,
        uw,
        um,
        us,
        dms.T,
        dss.T,
        ums.T,
        uss.T,
    )
    results = pl.pallas_call(
        deliver_kernel,
        out_shape=shapes,
        in_specs=[free] * 11,
        out_specs=(hbm,) * 11,
        scratch_shapes=[pltpu.VMEM(a.shape, a.dtype) for a in shapes] + [dma((17,)), dma((11,))],
        compiler_params=pltpu.CompilerParams(vmem_limit_bytes=60 << 20),
        name="deliver",
    )(*results)
    (layer, ndw, ndm, nds, nuw, num, nus, ndms, ndss, nums, nuss) = results
    return (layer, nuw, num, nums.T, nus, nuss.T, ndw, ndm, ndms.T, nds, ndss.T)


def per_device(
    tokens,
    counts,
    up_blocks,
    up_cols,
    down_blocks,
    down_rows,
    cotangent,
    up_moment,
    up_moment_scale,
    up_second,
    up_second_scale,
    down_moment,
    down_moment_scale,
    down_second,
    down_second_scale,
):
    return exchange(
        tokens,
        cotangent,
        counts,
        up_cols,
        down_rows,
        (up_blocks, up_moment, up_moment_scale, up_second, up_second_scale),
        (down_blocks, down_moment, down_moment_scale, down_second, down_second_scale),
    )


def solution(mesh):
    spread = P(("dp", "mp"), None)
    blocks = P("mp", None, None)
    table = P("mp", None)
    side = (blocks, blocks, table, blocks, table)
    return jax.shard_map(
        per_device,
        mesh=mesh,
        in_specs=(spread, P("dp"), blocks, table, blocks, table, spread)
        + (blocks, table, blocks, table) * 2,
        out_specs=(spread,) + side + side,
        check_vma=False,
    )
```

```python
import functools

import jax
import jax.numpy as jnp
from jax import lax
from jax.experimental import pallas as pl
from jax.experimental.pallas import tpu as pltpu
from jax.sharding import PartitionSpec as P

D = 8192
BLK = 128
COLS = D // BLK
K = 16
NZ = 16
NS = 8
NY = 4
ROWS = 128
QROWS = 16
GROUPS = 8
CODE_TOP = 32767.0
Z_PEERS = (8, 4, -4, 2, -2, 1, -1)

beta_one = 0.9
beta_two = 0.99
learn_rate = 0.002
decay_rate = 0.1
adam_eps = 1e-08
scale_eps = 1e-06
bias_one = 1.0 - 0.9**10
bias_two = 1.0 - 0.99**10

MESH = pl.DeviceIdType.MESH
F32 = jnp.float32
BF16 = jnp.bfloat16


def exchange_kernel(*refs):
    (tokens_hbm, cot_hbm, counts_hbm, cols_hbm, rows_hbm) = refs[:5]
    states_hbm = (refs[5:8], refs[8:11])
    scales_hbm = refs[11:15]
    layer_hbm = refs[15]
    new_hbm = (refs[16:19], refs[19:22])
    new_scales_hbm = refs[22:26]
    (
        tokens_ref,
        cot_ref,
        counts_ref,
        cols_ref,
        rows_ref,
        layer_ref,
        states_v,
        scales_s,
        scales_v,
        zbuf,
        rowtmp,
        turned,
        idx_v,
        idx_y,
        idx_s,
        pack,
        picked,
        cbuf,
        rs_recv,
        acc,
        zsend,
        hub_in,
        hub_out,
        zrecv,
        ypick,
        yact,
        gbuf,
        gscale,
        relay,
        rscale,
        grecv,
        gscale_in,
        gsum,
        gsum_scale,
        w_sem,
        i_sem,
        o_sem,
        zr_sem,
        s_sem,
        r_sem,
        gr_sem,
    ) = refs[26:]
    y = lax.axis_index("dp")
    mp = lax.axis_index("mp")
    z = mp // NS
    s = mp % NS

    def at_z(p):
        return (y, p * NS + s)

    def at_s(p):
        return (y, z * NS + p)

    def at_y(p):
        return (p, mp)

    def off(a, d, n):
        return (a + (d % n)) % n

    def remote(src, dst, ssem, rsem, dev):
        return pltpu.make_async_remote_copy(
            src_ref=src, dst_ref=dst, send_sem=ssem, recv_sem=rsem, device_id=dev, device_id_type=MESH
        )

    def arrived(part, sem):
        remote(part, part, sem, sem, at_y(off(y, 1, NY))).wait_recv()

    def left_here(part, sem):
        remote(part, part, sem, sem, at_y(off(y, 1, NY))).wait_send()

    barrier = pltpu.get_barrier_semaphore()
    for d in Z_PEERS:
        pl.semaphore_signal(barrier, inc=1, device_id=at_z(off(z, d, NZ)), device_id_type=MESH)
    for d in range(1, NS):
        pl.semaphore_signal(barrier, inc=1, device_id=at_s(off(s, d, NS)), device_id_type=MESH)
    for d in range(1, NY):
        pl.semaphore_signal(barrier, inc=1, device_id=at_y(off(y, d, NY)), device_id_type=MESH)

    loads = [
        pltpu.make_async_copy(src, dst, w_sem.at[i])
        for i, (src, dst) in enumerate(
            (
                (counts_hbm, counts_ref),
                (cols_hbm, cols_ref),
                (rows_hbm, rows_ref),
                (tokens_hbm, tokens_ref),
                (cot_hbm, cot_ref),
            )
        )
    ]
    state_loads = [
        [pltpu.make_async_copy(states_hbm[m][i], states_v.at[m, i], w_sem.at[5 + 2 * m + (i > 0)]) for i in range(3)]
        for m in range(2)
    ]
    scale_loads = [pltpu.make_async_copy(scales_hbm[i], scales_s.at[i], w_sem.at[9]) for i in range(4)]
    for copy in loads:
        copy.start()
    state_loads[1][0].start()
    state_loads[0][0].start()
    for copy in loads[:3]:
        copy.wait()

    valid = jnp.clip(counts_ref[0] - mp, 0, 1).astype(F32)

    sub = lax.broadcasted_iota(jnp.int32, (8, BLK), 0)
    lane = lax.broadcasted_iota(jnp.int32, (8, BLK), 1)
    tile = jnp.where(sub == 2, K, 0)
    for k in range(K):
        tile = jnp.where((sub == 0) & (lane == k), cols_ref[0, k], tile)
        tile = jnp.where((sub == 1) & (lane == k), rows_ref[0, k], tile)
        tile = jnp.where((sub == 2) & (lane == rows_ref[0, k]), k, tile)
    tile = jnp.where(sub == 3, counts_ref[0], tile)
    idx_v[s] = tile
    idx_y[0] = tile
    loads[3].wait()
    loads[4].wait()
    for m, ref in enumerate((tokens_ref, cot_ref)):
        for i in range(COLS):
            rowtmp[m * COLS + i : m * COLS + i + 1, :] = ref[0:1, i * BLK : (i + 1) * BLK].astype(F32)
    zbuf[z, 0:COLS, :] = rowtmp[0:COLS, :].astype(BF16)
    zbuf[z, COLS : 2 * COLS, :] = (rowtmp[COLS : 2 * COLS, :] * valid).astype(BF16)

    pl.semaphore_wait(barrier, len(Z_PEERS) + NS + NY - 2)

    def z_copy(m, w, p, o):
        part = zbuf.at[w, pl.ds(m * COLS, COLS), :]
        return remote(part, part, s_sem.at[0], zr_sem.at[m, o // 4 if o % 4 == 0 else 0], at_z(p))

    def z_start(m, h, e):
        z_copy(m, off(z, -h, NZ), off(z, e, NZ), (-h - e) % NZ).start()

    def z_wait(m, o):
        z_copy(m, off(z, o, NZ), off(z, 1, NZ), o).wait_recv()

    far = (8, 4, -4)
    near = ((2, 1, -1), (-2, 1, -1))

    for e in far:
        z_start(0, 0, e)
    for d in range(1, NS):
        remote(idx_v.at[s], idx_v.at[s], s_sem.at[1], r_sem.at[0], at_s(off(s, d, NS))).start()
    for d in range(1, NY):
        remote(idx_y.at[0], idx_y.at[d], s_sem.at[2], r_sem.at[1], at_y(off(y, d, NY))).start()
    for e in near[0]:
        z_start(0, 0, e)
    for e in far:
        z_start(1, 0, e)
    for m in range(2):
        state_loads[m][1].start()
        state_loads[m][2].start()
    for copy in scale_loads:
        copy.start()
    for ref in (gscale, rscale, gsum_scale, scales_v):
        ref[...] = jnp.zeros_like(ref)
    for src in range(NS):
        rs_recv[src, K] = jnp.zeros((QROWS, BLK), BF16)

    arrived(idx_v.at[pl.ds(0, NS - 1)], r_sem.at[0])
    to_smem = pltpu.make_async_copy(idx_v, idx_s, i_sem)
    to_smem.start()

    for h in (4, -4, 8):
        z_wait(0, (-h) % NZ)
        for e in near[0]:
            z_start(0, h, e)
    for e in near[1]:
        z_start(1, 0, e)
    for h in (4, -4, 8):
        z_wait(1, (-h) % NZ)
        for e in near[1]:
            z_start(1, h, e)

    flat = turned.reshape(2, COLS * NZ, BLK)

    to_smem.wait()

    def pack_and_send(m):
        arrived(zbuf.at[pl.ds(0, 6)], zr_sem.at[m, 0])
        for w in range(NZ):
            flat[m, pl.ds(w, COLS, stride=NZ), :] = zbuf[w, m * COLS : (m + 1) * COLS, :].astype(F32)

        def one(i, carry):
            d = (s + i) % NS
            for k in range(K):
                pack[m, i, k] = turned[m, idx_s[d, m, k]].astype(BF16)
            remote(pack.at[m, i], picked.at[m, s], s_sem.at[3], r_sem.at[2 + m], at_s(d)).start()
            return carry

        lax.fori_loop(1, NS, one, 0)
        for k in range(K):
            picked[m, s, k] = turned[m, idx_s[s, m, k]].astype(BF16)

    def wait_picked(m):
        arrived(picked.at[m, pl.ds(0, NS - 1)], r_sem.at[2 + m])
        return jnp.concatenate([picked[m, :, k].reshape(ROWS, BLK) for k in range(K)], axis=1)

    def y_copy(kind, d, p):
        if kind:
            src, dst = yact.at[0], yact.at[d]
        else:
            src, dst = picked.at[0, :, pl.ds(p * 4, 4)], ypick.at[d]
        return remote(src, dst, s_sem.at[7 + kind], r_sem.at[7 + kind], at_y(p))

    def y_send(kind):
        for d in range(1, NY):
            y_copy(kind, d, off(y, d, NY)).start()

    pack_and_send(0)
    pack_and_send(1)

    state_loads[1][0].wait()
    state_loads[0][0].wait()
    a_in = wait_picked(0)
    y_send(0)
    up_wide = jnp.concatenate([states_v[1, 0, k] for k in range(K)], axis=1)
    preact = lax.dot_general(a_in, up_wide, (((1,), (1,)), ((), ())), preferred_element_type=F32)
    squash = 1.0 / (1.0 + jnp.exp(-preact))
    hidden = (preact * squash).astype(BF16)
    down_tall = states_v[0, 0].reshape(K * BLK, BLK)
    contrib = lax.dot_general(hidden, down_tall, (((1,), (1,)), ((), ())), preferred_element_type=F32)
    for k in range(K):
        cbuf[:, k] = contrib[:, k * BLK : (k + 1) * BLK].astype(BF16).reshape(NS, QROWS, BLK)
    for d in range(1, NS):
        p = off(s, d, NS)
        remote(
            cbuf.at[p], rs_recv.at[s, pl.ds(0, K)], s_sem.at[4], r_sem.at[4], at_s(p)
        ).start()
    rs_recv[s, 0:K] = cbuf[s]

    def coded(grad):
        top = jnp.max(jnp.abs(grad), axis=0, keepdims=True)
        code = jnp.round(grad * (CODE_TOP / jnp.maximum(top, 1e-30)))
        return code.astype(jnp.int32).astype(jnp.int16), top * (1.0 / CODE_TOP)

    left, right, across = off(y, -1, NY), off(y, 1, NY), off(y, 2, NY)

    def grad_msg(m, msg, at, p):
        part, scales = gsum.at[at], gsum_scale.at[at]
        return (
            remote(part, part, s_sem.at[9], gr_sem.at[m, msg], at_y(p)),
            remote(scales, scales, s_sem.at[10], gr_sem.at[m, 6 + msg], at_y(p)),
        )

    def grad_out(m, msg):
        at = ((m, y, 1), (m, y, 0), (m, left, 1), (m, right, 0), (m, y, 0), (m, y, 1))[msg]
        return grad_msg(m, msg, at, (right, left)[msg % 2])

    def grad_send(m, *msgs):
        for msg in msgs:
            for copy in grad_out(m, msg):
                copy.start()

    def grad_back(m, msg):
        at = ((m, left, 1), (m, right, 0), (m, across, 1), (m, across, 0), (m, left, 0), (m, right, 1))[msg]
        for copy in grad_msg(m, msg, at, left):
            copy.wait_recv()

    def own_store(m, half, b, total):
        code, scale = coded(total * per_token)
        gsum[m, y, half, b] = code
        gsum_scale[m, y, half, b : b + 1, :] = scale

    def own_up():
        arrived(yact.at[pl.ds(0, NY - 1)], r_sem.at[8])
        arrived(ypick.at[pl.ds(0, NY - 1)], r_sem.at[7])
        total = None
        for d in range(NY):
            if d:
                wide = jnp.concatenate([ypick[d, :, k].reshape(ROWS, BLK) for k in range(4)], axis=1)
            else:
                wide = jnp.concatenate([picked[0, :, y * 4 + k].reshape(ROWS, BLK) for k in range(4)], axis=1)
            part = lax.dot_general(yact[d], wide, (((0,), (0,)), ((), ())), preferred_element_type=F32)
            total = part if total is None else total + part
        for k in range(4):
            own_store(1, k // 2, k % 2, total[:, k * BLK : (k + 1) * BLK])

    def ring(msg):
        if msg < 4:
            at = ((across, 1), (across, 0), (right, 0), (left, 1))[msg]
            src, scl = gbuf.at[at], gscale.at[at]
        else:
            src, scl = relay.at[5 - msg], rscale.at[5 - msg]
        to = at_y((right, left)[msg % 2])
        r = 11 if msg < 2 else 13
        return (
            remote(src, grecv.at[msg], s_sem.at[11], r_sem.at[r], to),
            remote(scl, gscale_in.at[msg], s_sem.at[12], r_sem.at[r + 1], to),
        )

    def ring_send(*msgs):
        for msg in msgs:
            for copy in ring(msg):
                copy.start()

    def own_value(q, half, b):
        return gbuf[q, half, b].astype(F32) * gscale[q, half, b : b + 1, :]

    def came(msg, b):
        return grecv[msg, b].astype(F32) * gscale_in[msg, b : b + 1, :]

    def ring_pass():
        arrived(grecv.at[pl.ds(0, 2)], r_sem.at[11])
        arrived(gscale_in.at[pl.ds(0, 2)], r_sem.at[12])
        for msg, q in ((0, right), (1, left)):
            for b in range(2):
                code, scale = coded(came(msg, b) + own_value(q, 1 - msg, b))
                relay[1 - msg, b] = code
                rscale[1 - msg, b : b + 1, :] = scale
        ring_send(4, 5)

    def own_down():
        arrived(grecv.at[pl.ds(2, 4)], r_sem.at[13])
        arrived(gscale_in.at[pl.ds(2, 4)], r_sem.at[14])
        for half in range(2):
            for b in range(2):
                own_store(0, half, b, own_value(y, half, b) + came(2 + half, b) + came(5 - half, b))

    lane = lax.broadcasted_iota(jnp.int32, (8, K), 1)

    def adam(m, q):
        def block_step(i, carry):
            half, b = i // 2, i % 2
            block = q * 4 + i
            g_scale = gsum_scale[m, q, half, pl.ds(b, 1), :]
            moments, seconds = [], []
            for g in range(GROUPS):
                rows = slice(g * QROWS, (g + 1) * QROWS)
                grad = gsum[m, q, half, b, rows, :].astype(F32) * g_scale
                m_scale = beta_one * scales_s[2 * m, g, block]
                s_scale = beta_two * scales_s[2 * m + 1, g, block]
                m_new = m_scale * states_v[m, 1, block, rows, :].astype(F32) + (1.0 - beta_one) * grad
                s_new = s_scale * states_v[m, 2, block, rows, :].astype(F32) + (1.0 - beta_two) * (grad * grad)
                second = s_new * (1.0 / bias_two)
                root = second * lax.rsqrt(second) + adam_eps
                w_old = states_v[m, 0, block, rows, :].astype(F32)
                w_new = w_old * (1.0 - learn_rate * decay_rate) - (m_new * (learn_rate / bias_one)) * pl.reciprocal(
                    root, approx=True
                )
                states_v[m, 0, block, rows, :] = w_new.astype(BF16)
                moments.append(m_new)
                seconds.append(s_new)
            for j, values in ((0, moments), (1, seconds)):
                tops = jnp.concatenate([jnp.max(jnp.abs(v), axis=0, keepdims=True) for v in values], axis=0)
                top = jnp.max(tops, axis=1, keepdims=True) + scale_eps
                inverse = jnp.broadcast_to(1.0 / top, (8, BLK))
                for g in range(GROUPS):
                    rows = slice(g * QROWS, (g + 1) * QROWS)
                    states_v[m, 1 + j, block, rows, :] = (values[g] * inverse[g : g + 1, :]).astype(BF16)
                scales_v[2 * m + j] = jnp.where(lane == block, top, scales_v[2 * m + j])
            return carry

        lax.fori_loop(0, 4, block_step, 0)
        for i in range(3):
            out_copy(m, q, i).start()

    def out_copy(m, q, i):
        rows = pl.ds(q * 4, 4)
        return pltpu.make_async_copy(states_v.at[m, i, rows], new_hbm[m][i].at[rows], o_sem)

    cot_in = wait_picked(1)
    down_grad = lax.dot_general(cot_in, hidden, (((0,), (0,)), ((), ())), preferred_element_type=F32)
    for k in range(K):
        code, scale = coded(down_grad[k * BLK : (k + 1) * BLK, :])
        gbuf[k // 4, k // 2 % 2, k % 2] = code
        gscale[k // 4, k // 2 % 2, k % 2 : k % 2 + 1, :] = scale
    ring_send(0, 1)
    hidden_grad = jnp.dot(cot_in, down_tall, preferred_element_type=F32)
    yact[0] = (hidden_grad * squash * (1.0 + preact * (1.0 - squash))).astype(BF16)
    y_send(1)
    ring_send(2, 3)

    left_here(zbuf.at[pl.ds(0, NZ - 1)], s_sem.at[0])
    left_here(idx_v.at[pl.ds(0, NS - 1)], s_sem.at[1])
    left_here(idx_y.at[pl.ds(0, NY - 1)], s_sem.at[2])
    left_here(pack.at[:, pl.ds(1, NS - 1)], s_sem.at[3])
    arrived(idx_y.at[pl.ds(0, NY - 1)], r_sem.at[1])
    count = idx_y[0, 3:4, :]
    for d in range(1, NY):
        count = count + idx_y[d, 3:4, :]
    per_token = 1.0 / count.astype(F32)

    ring_pass()

    arrived(cbuf.at[pl.ds(0, NS - 1)], r_sem.at[4])

    def gather_rows(r, carry):
        total = rs_recv[0, idx_s[0, 2, r]].astype(F32)
        for src in range(1, NS):
            total = total + rs_recv[src, idx_s[src, 2, r]].astype(F32)
        acc[pl.ds(pl.multiple_of(r * NZ, NZ), NZ), :] = total
        return carry

    lax.fori_loop(0, COLS, gather_rows, 0)
    for w in range(NZ):
        zsend[w % 4, w // 4] = acc[pl.ds(w, COLS, stride=NZ), :].astype(BF16)

    core = s % 2
    hubs = (off(z + 12 * core, 2, NZ), off(z, 1, NZ), off(z, -1, NZ))

    def hub_copy(j, p):
        return remote(zsend.at[p % 4], hub_in.at[j], s_sem.at[5], r_sem.at[5], at_z(p))

    def row_copy(j, p):
        return remote(hub_out.at[p // 4], zrecv.at[j], s_sem.at[6], r_sem.at[6], at_z(p))

    for j in range(3):
        hub_copy(j, hubs[j]).start()

    for m in range(2):
        both = states_v.at[m, pl.ds(1, 2)]
        pltpu.make_async_copy(both, both, w_sem.at[6 + 2 * m]).wait()
    pltpu.make_async_copy(scales_s, scales_s, w_sem.at[9]).wait()
    own_up()
    grad_send(1, 0, 1, 4, 5)
    adam(1, y)
    own_down()
    grad_send(0, 0, 1, 4, 5)
    adam(0, y)

    arrived(hub_in, r_sem.at[5])
    for w in range(4):
        part = zsend[z % 4, w].astype(F32)
        for j in range(3):
            part = part + hub_in[j, w].astype(F32)
        hub_out[w] = part.astype(BF16)
    for j in (2, 1, 3):
        row_copy(j, off(z, 4 * j, NZ)).start()

    grad_back(1, 0)
    grad_send(1, 2)
    grad_back(1, 1)
    grad_send(1, 3)
    grad_back(1, 4)
    adam(1, left)
    grad_back(1, 5)
    adam(1, right)
    grad_back(0, 0)
    grad_send(0, 2)
    grad_back(0, 1)
    grad_send(0, 3)
    grad_back(0, 4)
    adam(0, left)
    grad_back(0, 5)
    adam(0, right)
    grad_back(1, 2)
    grad_back(1, 3)
    adam(1, across)
    arrived(hub_out.at[pl.ds(0, 3)], r_sem.at[6])
    row = hub_out[z // 4].astype(F32)
    for j in (1, 2, 3):
        row = row + zrecv[j].astype(F32)
    row = row * valid
    for i in range(COLS):
        layer_ref[0:1, i * BLK : (i + 1) * BLK] = row[i : i + 1, :].astype(BF16)
    layer_out = pltpu.make_async_copy(layer_ref, layer_hbm, w_sem.at[0])
    layer_out.start()
    left_here(hub_in, s_sem.at[5])
    left_here(hub_out.at[pl.ds(0, 3)], s_sem.at[6])
    left_here(cbuf.at[pl.ds(0, NS - 1)], s_sem.at[4])
    left_here(ypick.at[pl.ds(0, NY - 1)], s_sem.at[7])
    left_here(yact.at[pl.ds(0, NY - 1)], s_sem.at[8])
    left_here(grecv, s_sem.at[11])
    left_here(gscale_in, s_sem.at[12])
    grad_back(0, 2)
    grad_back(0, 3)
    adam(0, across)
    scale_out = [pltpu.make_async_copy(scales_v.at[i], new_scales_hbm[i], w_sem.at[1]) for i in range(4)]
    for copy in scale_out:
        copy.start()
    left_here(gsum.at[:, pl.ds(0, 3)], s_sem.at[9])
    left_here(gsum_scale.at[:, pl.ds(0, 3)], s_sem.at[10])
    layer_out.wait()
    pltpu.make_async_copy(states_v, states_v, o_sem).wait()
    pltpu.make_async_copy(scales_v, scales_v, w_sem.at[1]).wait()


def deliver_kernel(*refs):
    n = 11
    held, in_sem, out_sem = refs[2 * n : 3 * n], refs[3 * n], refs[3 * n + 1]
    parts = []
    for i in range(n):
        if len(refs[i].shape) == 3:
            parts += [(i, pl.ds(0, K // 2)), (i, pl.ds(K // 2, K // 2))]
        else:
            parts.append((i, pl.ds(0, refs[i].shape[0])))
    loads = [pltpu.make_async_copy(refs[i].at[at], held[i].at[at], in_sem.at[j]) for j, (i, at) in enumerate(parts)]
    stores = [
        pltpu.make_async_copy(held[i].at[at], refs[n + i].at[at], out_sem.at[i]) for i, at in parts
    ]
    for load in loads:
        load.start()
    for load, store in zip(loads, stores):
        load.wait()
        store.start()
    for i in range(n):
        pltpu.make_async_copy(held[i], refs[n + i], out_sem.at[i]).wait()


def exchange(tokens, cotangent, counts, up_cols, down_rows, up, down):
    hbm = pl.BlockSpec(memory_space=pltpu.HBM)
    free = pl.BlockSpec(memory_space=pl.ANY)
    dma = pltpu.SemaphoreType.DMA
    (uw, um, ums, us, uss) = up
    (dw, dm, dms, ds, dss) = down
    big = jax.ShapeDtypeStruct((K, BLK, BLK), BF16)
    small = jax.ShapeDtypeStruct((GROUPS, K), F32)
    shapes = (jax.ShapeDtypeStruct((1, D), BF16),) + (big,) * 6 + (small,) * 4
    results = pl.pallas_call(
        exchange_kernel,
        out_shape=shapes,
        in_specs=[hbm] * 15,
        out_specs=(free,) * 11,
        scratch_shapes=[
            pltpu.VMEM((1, D), BF16),
            pltpu.VMEM((1, D), BF16),
            pltpu.SMEM((1,), jnp.int32),
            pltpu.SMEM((1, K), jnp.int32),
            pltpu.SMEM((1, K), jnp.int32),
            pltpu.VMEM((1, D), BF16),
            pltpu.VMEM((2, 3, K, BLK, BLK), BF16),
            pltpu.SMEM((4, GROUPS, K), F32),
            pltpu.VMEM((4, GROUPS, K), F32),
            pltpu.VMEM((NZ, 2 * COLS, BLK), BF16),
            pltpu.VMEM((2 * COLS, BLK), F32),
            pltpu.VMEM((2, COLS, NZ, BLK), F32),
            pltpu.VMEM((NS, 8, BLK), jnp.int32),
            pltpu.VMEM((NY, 8, BLK), jnp.int32),
            pltpu.SMEM((NS, 8, BLK), jnp.int32),
            pltpu.VMEM((2, NS, K, QROWS, BLK), BF16),
            pltpu.VMEM((2, NS, K, QROWS, BLK), BF16),
            pltpu.VMEM((NS, K, QROWS, BLK), BF16),
            pltpu.VMEM((NS, K + 1, QROWS, BLK), BF16),
            pltpu.VMEM((COLS * NZ, BLK), F32),
            pltpu.VMEM((4, 4, COLS, BLK), BF16),
            pltpu.VMEM((3, 4, COLS, BLK), BF16),
            pltpu.VMEM((4, COLS, BLK), BF16),
            pltpu.VMEM((4, COLS, BLK), BF16),
            pltpu.VMEM((NY, NS, 4, QROWS, BLK), BF16),
            pltpu.VMEM((NY, ROWS, BLK), BF16),
            pltpu.VMEM((NY, 2, 2, BLK, BLK), jnp.int16),
            pltpu.VMEM((NY, 2, 8, BLK), F32),
            pltpu.VMEM((2, 2, BLK, BLK), jnp.int16),
            pltpu.VMEM((2, 8, BLK), F32),
            pltpu.VMEM((6, 2, BLK, BLK), jnp.int16),
            pltpu.VMEM((6, 8, BLK), F32),
            pltpu.VMEM((2, NY, 2, 2, BLK, BLK), jnp.int16),
            pltpu.VMEM((2, NY, 2, 8, BLK), F32),
            dma((10,)),
            dma,
            dma,
            dma((2, 4)),
            dma((13,)),
            dma((15,)),
            dma((2, 12)),
        ],
        compiler_params=pltpu.CompilerParams(
            collective_id=1, has_side_effects=True, vmem_limit_bytes=60 << 20
        ),
        cost_estimate=pl.CostEstimate(flops=400_000_000, bytes_accessed=8 << 20, transcendentals=1_000_000),
        name="exchange",
    )(
        tokens,
        cotangent,
        counts,
        up_cols,
        down_rows,
        dw,
        dm,
        ds,
        uw,
        um,
        us,
        dms.T,
        dss.T,
        ums.T,
        uss.T,
    )
    results = pl.pallas_call(
        deliver_kernel,
        out_shape=shapes,
        in_specs=[free] * 11,
        out_specs=(hbm,) * 11,
        scratch_shapes=[pltpu.VMEM(a.shape, a.dtype) for a in shapes] + [dma((17,)), dma((11,))],
        compiler_params=pltpu.CompilerParams(vmem_limit_bytes=60 << 20),
        name="deliver",
    )(*results)
    (layer, ndw, ndm, nds, nuw, num, nus, ndms, ndss, nums, nuss) = results
    return (layer, nuw, num, nums.T, nus, nuss.T, ndw, ndm, ndms.T, nds, ndss.T)


def per_device(
    tokens,
    counts,
    up_blocks,
    up_cols,
    down_blocks,
    down_rows,
    cotangent,
    up_moment,
    up_moment_scale,
    up_second,
    up_second_scale,
    down_moment,
    down_moment_scale,
    down_second,
    down_second_scale,
):
    return exchange(
        tokens,
        cotangent,
        counts,
        up_cols,
        down_rows,
        (up_blocks, up_moment, up_moment_scale, up_second, up_second_scale),
        (down_blocks, down_moment, down_moment_scale, down_second, down_second_scale),
    )


def solution(mesh):
    spread = P(("dp", "mp"), None)
    blocks = P("mp", None, None)
    table = P("mp", None)
    side = (blocks, blocks, table, blocks, table)
    return jax.shard_map(
        per_device,
        mesh=mesh,
        in_specs=(spread, P("dp"), blocks, table, blocks, table, spread)
        + (blocks, table, blocks, table) * 2,
        out_specs=(spread,) + side + side,
        check_vma=False,
    )
```

```python
import functools

import jax
import jax.numpy as jnp
from jax import lax
from jax.experimental import pallas as pl
from jax.experimental.pallas import tpu as pltpu
from jax.sharding import PartitionSpec as P

D = 8192
BLK = 128
COLS = D // BLK
K = 16
NZ = 16
NS = 8
NY = 4
ROWS = 128
QROWS = 16
GROUPS = 8
CODE_TOP = 32767.0
Z_PEERS = (8, 4, -4, 2, -2, 1, -1)

beta_one = 0.9
beta_two = 0.99
learn_rate = 0.002
decay_rate = 0.1
adam_eps = 1e-08
scale_eps = 1e-06
bias_one = 1.0 - 0.9**10
bias_two = 1.0 - 0.99**10

MESH = pl.DeviceIdType.MESH
F32 = jnp.float32
BF16 = jnp.bfloat16


def exchange_kernel(*refs):
    (tokens_hbm, cot_hbm, counts_hbm, cols_hbm, rows_hbm) = refs[:5]
    states_hbm = (refs[5:8], refs[8:11])
    scales_hbm = refs[11:15]
    layer_hbm = refs[15]
    new_hbm = (refs[16:19], refs[19:22])
    new_scales_hbm = refs[22:26]
    (
        tokens_ref,
        cot_ref,
        counts_ref,
        cols_ref,
        rows_ref,
        layer_ref,
        states_v,
        scales_s,
        scales_v,
        zbuf,
        rowtmp,
        turned,
        idx_v,
        idx_y,
        idx_s,
        pack,
        picked,
        cbuf,
        rs_recv,
        acc,
        zsend,
        hub_in,
        hub_out,
        zrecv,
        ypick,
        yact,
        gbuf,
        gscale,
        relay,
        rscale,
        grecv,
        gscale_in,
        gsum,
        gsum_scale,
        w_sem,
        i_sem,
        o_sem,
        zr_sem,
        s_sem,
        r_sem,
        gr_sem,
    ) = refs[26:]
    y = lax.axis_index("dp")
    mp = lax.axis_index("mp")
    z = mp // NS
    s = mp % NS

    def at_z(p):
        return (y, p * NS + s)

    def at_s(p):
        return (y, z * NS + p)

    def at_y(p):
        return (p, mp)

    def off(a, d, n):
        return (a + (d % n)) % n

    def remote(src, dst, ssem, rsem, dev):
        return pltpu.make_async_remote_copy(
            src_ref=src, dst_ref=dst, send_sem=ssem, recv_sem=rsem, device_id=dev, device_id_type=MESH
        )

    def arrived(part, sem):
        remote(part, part, sem, sem, at_y(off(y, 1, NY))).wait_recv()

    def left_here(part, sem):
        remote(part, part, sem, sem, at_y(off(y, 1, NY))).wait_send()

    barrier = pltpu.get_barrier_semaphore()
    for d in Z_PEERS:
        pl.semaphore_signal(barrier, inc=1, device_id=at_z(off(z, d, NZ)), device_id_type=MESH)
    for d in range(1, NS):
        pl.semaphore_signal(barrier, inc=1, device_id=at_s(off(s, d, NS)), device_id_type=MESH)
    for d in range(1, NY):
        pl.semaphore_signal(barrier, inc=1, device_id=at_y(off(y, d, NY)), device_id_type=MESH)

    loads = [
        pltpu.make_async_copy(src, dst, w_sem.at[i])
        for i, (src, dst) in enumerate(
            (
                (counts_hbm, counts_ref),
                (cols_hbm, cols_ref),
                (rows_hbm, rows_ref),
                (tokens_hbm, tokens_ref),
                (cot_hbm, cot_ref),
            )
        )
    ]
    state_loads = [
        [pltpu.make_async_copy(states_hbm[m][i], states_v.at[m, i], w_sem.at[5 + 2 * m + (i > 0)]) for i in range(3)]
        for m in range(2)
    ]
    scale_loads = [pltpu.make_async_copy(scales_hbm[i], scales_s.at[i], w_sem.at[9]) for i in range(4)]
    for copy in loads:
        copy.start()
    state_loads[1][0].start()
    state_loads[0][0].start()
    for copy in loads[:3]:
        copy.wait()

    valid = jnp.clip(counts_ref[0] - mp, 0, 1).astype(F32)

    sub = lax.broadcasted_iota(jnp.int32, (8, BLK), 0)
    lane = lax.broadcasted_iota(jnp.int32, (8, BLK), 1)
    tile = jnp.where(sub == 2, K, 0)
    for k in range(K):
        tile = jnp.where((sub == 0) & (lane == k), cols_ref[0, k], tile)
        tile = jnp.where((sub == 1) & (lane == k), rows_ref[0, k], tile)
        tile = jnp.where((sub == 2) & (lane == rows_ref[0, k]), k, tile)
    tile = jnp.where(sub == 3, counts_ref[0], tile)
    idx_v[s] = tile
    idx_y[0] = tile
    loads[3].wait()
    loads[4].wait()
    for m, ref in enumerate((tokens_ref, cot_ref)):
        for i in range(COLS):
            rowtmp[m * COLS + i : m * COLS + i + 1, :] = ref[0:1, i * BLK : (i + 1) * BLK].astype(F32)
    zbuf[z, 0:COLS, :] = rowtmp[0:COLS, :].astype(BF16)
    zbuf[z, COLS : 2 * COLS, :] = (rowtmp[COLS : 2 * COLS, :] * valid).astype(BF16)

    pl.semaphore_wait(barrier, len(Z_PEERS) + NS + NY - 2)

    def z_copy(m, w, p, o):
        part = zbuf.at[w, pl.ds(m * COLS, COLS), :]
        return remote(part, part, s_sem.at[0], zr_sem.at[m, o // 4 if o % 4 == 0 else 0], at_z(p))

    def z_start(m, h, e):
        z_copy(m, off(z, -h, NZ), off(z, e, NZ), (-h - e) % NZ).start()

    def z_wait(m, o):
        z_copy(m, off(z, o, NZ), off(z, 1, NZ), o).wait_recv()

    far = (8, 4, -4)
    near = ((2, 1, -1), (-2, 1, -1))

    for e in far:
        z_start(0, 0, e)
    for d in range(1, NS):
        remote(idx_v.at[s], idx_v.at[s], s_sem.at[1], r_sem.at[0], at_s(off(s, d, NS))).start()
    for d in range(1, NY):
        remote(idx_y.at[0], idx_y.at[d], s_sem.at[2], r_sem.at[1], at_y(off(y, d, NY))).start()
    for e in near[0]:
        z_start(0, 0, e)
    for e in far:
        z_start(1, 0, e)
    for m in range(2):
        state_loads[m][1].start()
        state_loads[m][2].start()
    for copy in scale_loads:
        copy.start()
    for ref in (gscale, rscale, gsum_scale, scales_v):
        ref[...] = jnp.zeros_like(ref)
    for src in range(NS):
        rs_recv[src, K] = jnp.zeros((QROWS, BLK), BF16)

    arrived(idx_v.at[pl.ds(0, NS - 1)], r_sem.at[0])
    to_smem = pltpu.make_async_copy(idx_v, idx_s, i_sem)
    to_smem.start()

    for h in (4, -4, 8):
        z_wait(0, (-h) % NZ)
        for e in near[0]:
            z_start(0, h, e)
    for e in near[1]:
        z_start(1, 0, e)
    for h in (4, -4, 8):
        z_wait(1, (-h) % NZ)
        for e in near[1]:
            z_start(1, h, e)

    flat = turned.reshape(2, COLS * NZ, BLK)

    to_smem.wait()

    def pack_and_send(m):
        arrived(zbuf.at[pl.ds(0, 6)], zr_sem.at[m, 0])
        for w in range(NZ):
            flat[m, pl.ds(w, COLS, stride=NZ), :] = zbuf[w, m * COLS : (m + 1) * COLS, :].astype(F32)

        def one(turn, carry):
            i = (turn + 1) % (NS - 1) + 1
            d = (s + i) % NS
            for k in range(K):
                pack[m, i, k] = turned[m, idx_s[d, m, k]].astype(BF16)
            remote(pack.at[m, i], picked.at[m, s], s_sem.at[3], r_sem.at[2 + m], at_s(d)).start()
            return carry

        lax.fori_loop(1, NS, one, 0)
        for k in range(K):
            picked[m, s, k] = turned[m, idx_s[s, m, k]].astype(BF16)

    def wait_picked(m):
        arrived(picked.at[m, pl.ds(0, NS - 1)], r_sem.at[2 + m])
        return jnp.concatenate([picked[m, :, k].reshape(ROWS, BLK) for k in range(K)], axis=1)

    def y_copy(kind, d, p):
        if kind:
            src, dst = yact.at[0], yact.at[d]
        else:
            src, dst = picked.at[0, :, pl.ds(p * 4, 4)], ypick.at[d]
        return remote(src, dst, s_sem.at[7 + kind], r_sem.at[7 + kind], at_y(p))

    def y_send(kind):
        for d in range(1, NY):
            y_copy(kind, d, off(y, d, NY)).start()

    pack_and_send(0)
    pack_and_send(1)

    state_loads[1][0].wait()
    state_loads[0][0].wait()
    a_in = wait_picked(0)
    y_send(0)
    up_wide = jnp.concatenate([states_v[1, 0, k] for k in range(K)], axis=1)
    preact = lax.dot_general(a_in, up_wide, (((1,), (1,)), ((), ())), preferred_element_type=F32)
    squash = 1.0 / (1.0 + jnp.exp(-preact))
    hidden = (preact * squash).astype(BF16)
    down_tall = states_v[0, 0].reshape(K * BLK, BLK)
    contrib = lax.dot_general(hidden, down_tall, (((1,), (1,)), ((), ())), preferred_element_type=F32)
    for k in range(K):
        cbuf[:, k] = contrib[:, k * BLK : (k + 1) * BLK].astype(BF16).reshape(NS, QROWS, BLK)
    for d in (4, 3, 5, 2, 6, 1, 7):
        p = off(s, d, NS)
        remote(
            cbuf.at[p], rs_recv.at[s, pl.ds(0, K)], s_sem.at[4], r_sem.at[4], at_s(p)
        ).start()
    rs_recv[s, 0:K] = cbuf[s]

    def coded(grad):
        top = jnp.max(jnp.abs(grad), axis=0, keepdims=True)
        code = jnp.round(grad * (CODE_TOP / jnp.maximum(top, 1e-30)))
        return code.astype(jnp.int32).astype(jnp.int16), top * (1.0 / CODE_TOP)

    left, right, across = off(y, -1, NY), off(y, 1, NY), off(y, 2, NY)

    def grad_msg(m, msg, at, p):
        part, scales = gsum.at[at], gsum_scale.at[at]
        return (
            remote(part, part, s_sem.at[9], gr_sem.at[m, msg], at_y(p)),
            remote(scales, scales, s_sem.at[10], gr_sem.at[m, 6 + msg], at_y(p)),
        )

    def grad_out(m, msg):
        at = ((m, y, 1), (m, y, 0), (m, left, 1), (m, right, 0), (m, y, 0), (m, y, 1))[msg]
        return grad_msg(m, msg, at, (right, left)[msg % 2])

    def grad_send(m, *msgs):
        for msg in msgs:
            for copy in grad_out(m, msg):
                copy.start()

    def grad_back(m, msg):
        at = ((m, left, 1), (m, right, 0), (m, across, 1), (m, across, 0), (m, left, 0), (m, right, 1))[msg]
        for copy in grad_msg(m, msg, at, left):
            copy.wait_recv()

    def own_store(m, half, b, total):
        code, scale = coded(total * per_token)
        gsum[m, y, half, b] = code
        gsum_scale[m, y, half, b : b + 1, :] = scale

    def own_up():
        arrived(yact.at[pl.ds(0, NY - 1)], r_sem.at[8])
        arrived(ypick.at[pl.ds(0, NY - 1)], r_sem.at[7])
        total = None
        for d in range(NY):
            if d:
                wide = jnp.concatenate([ypick[d, :, k].reshape(ROWS, BLK) for k in range(4)], axis=1)
            else:
                wide = jnp.concatenate([picked[0, :, y * 4 + k].reshape(ROWS, BLK) for k in range(4)], axis=1)
            part = lax.dot_general(yact[d], wide, (((0,), (0,)), ((), ())), preferred_element_type=F32)
            total = part if total is None else total + part
        for k in range(4):
            own_store(1, k // 2, k % 2, total[:, k * BLK : (k + 1) * BLK])

    def ring(msg):
        if msg < 4:
            at = ((across, 1), (across, 0), (right, 0), (left, 1))[msg]
            src, scl = gbuf.at[at], gscale.at[at]
        else:
            src, scl = relay.at[5 - msg], rscale.at[5 - msg]
        to = at_y((right, left)[msg % 2])
        r = 11 if msg < 2 else 13
        return (
            remote(src, grecv.at[msg], s_sem.at[11], r_sem.at[r], to),
            remote(scl, gscale_in.at[msg], s_sem.at[12], r_sem.at[r + 1], to),
        )

    def ring_send(*msgs):
        for msg in msgs:
            for copy in ring(msg):
                copy.start()

    def own_value(q, half, b):
        return gbuf[q, half, b].astype(F32) * gscale[q, half, b : b + 1, :]

    def came(msg, b):
        return grecv[msg, b].astype(F32) * gscale_in[msg, b : b + 1, :]

    def ring_pass():
        arrived(grecv.at[pl.ds(0, 2)], r_sem.at[11])
        arrived(gscale_in.at[pl.ds(0, 2)], r_sem.at[12])
        for msg, q in ((0, right), (1, left)):
            for b in range(2):
                code, scale = coded(came(msg, b) + own_value(q, 1 - msg, b))
                relay[1 - msg, b] = code
                rscale[1 - msg, b : b + 1, :] = scale
        ring_send(4, 5)

    def own_down():
        arrived(grecv.at[pl.ds(2, 4)], r_sem.at[13])
        arrived(gscale_in.at[pl.ds(2, 4)], r_sem.at[14])
        for half in range(2):
            for b in range(2):
                own_store(0, half, b, own_value(y, half, b) + came(2 + half, b) + came(5 - half, b))

    lane = lax.broadcasted_iota(jnp.int32, (8, K), 1)

    def adam(m, q):
        def block_step(i, carry):
            half, b = i // 2, i % 2
            block = q * 4 + i
            g_scale = gsum_scale[m, q, half, pl.ds(b, 1), :]
            moments, seconds = [], []
            for g in range(GROUPS):
                rows = slice(g * QROWS, (g + 1) * QROWS)
                grad = gsum[m, q, half, b, rows, :].astype(F32) * g_scale
                m_scale = beta_one * scales_s[2 * m, g, block]
                s_scale = beta_two * scales_s[2 * m + 1, g, block]
                m_new = m_scale * states_v[m, 1, block, rows, :].astype(F32) + (1.0 - beta_one) * grad
                s_new = s_scale * states_v[m, 2, block, rows, :].astype(F32) + (1.0 - beta_two) * (grad * grad)
                second = s_new * (1.0 / bias_two)
                root = second * lax.rsqrt(second) + adam_eps
                w_old = states_v[m, 0, block, rows, :].astype(F32)
                w_new = w_old * (1.0 - learn_rate * decay_rate) - (m_new * (learn_rate / bias_one)) * pl.reciprocal(
                    root, approx=True
                )
                states_v[m, 0, block, rows, :] = w_new.astype(BF16)
                moments.append(m_new)
                seconds.append(s_new)
            for j, values in ((0, moments), (1, seconds)):
                tops = jnp.concatenate([jnp.max(jnp.abs(v), axis=0, keepdims=True) for v in values], axis=0)
                top = jnp.max(tops, axis=1, keepdims=True) + scale_eps
                inverse = jnp.broadcast_to(1.0 / top, (8, BLK))
                for g in range(GROUPS):
                    rows = slice(g * QROWS, (g + 1) * QROWS)
                    states_v[m, 1 + j, block, rows, :] = (values[g] * inverse[g : g + 1, :]).astype(BF16)
                scales_v[2 * m + j] = jnp.where(lane == block, top, scales_v[2 * m + j])
            return carry

        lax.fori_loop(0, 4, block_step, 0)
        for i in range(3):
            out_copy(m, q, i).start()

    def out_copy(m, q, i):
        rows = pl.ds(q * 4, 4)
        return pltpu.make_async_copy(states_v.at[m, i, rows], new_hbm[m][i].at[rows], o_sem)

    cot_in = wait_picked(1)
    down_grad = lax.dot_general(cot_in, hidden, (((0,), (0,)), ((), ())), preferred_element_type=F32)
    for k in range(K):
        code, scale = coded(down_grad[k * BLK : (k + 1) * BLK, :])
        gbuf[k // 4, k // 2 % 2, k % 2] = code
        gscale[k // 4, k // 2 % 2, k % 2 : k % 2 + 1, :] = scale
    ring_send(0, 1)
    hidden_grad = jnp.dot(cot_in, down_tall, preferred_element_type=F32)
    yact[0] = (hidden_grad * squash * (1.0 + preact * (1.0 - squash))).astype(BF16)
    y_send(1)
    ring_send(2, 3)

    left_here(zbuf.at[pl.ds(0, NZ - 1)], s_sem.at[0])
    left_here(idx_v.at[pl.ds(0, NS - 1)], s_sem.at[1])
    left_here(idx_y.at[pl.ds(0, NY - 1)], s_sem.at[2])
    left_here(pack.at[:, pl.ds(1, NS - 1)], s_sem.at[3])
    arrived(idx_y.at[pl.ds(0, NY - 1)], r_sem.at[1])
    count = idx_y[0, 3:4, :]
    for d in range(1, NY):
        count = count + idx_y[d, 3:4, :]
    per_token = 1.0 / count.astype(F32)

    ring_pass()

    arrived(cbuf.at[pl.ds(0, NS - 1)], r_sem.at[4])

    def gather_rows(r, carry):
        total = rs_recv[0, idx_s[0, 2, r]].astype(F32)
        for src in range(1, NS):
            total = total + rs_recv[src, idx_s[src, 2, r]].astype(F32)
        acc[pl.ds(pl.multiple_of(r * NZ, NZ), NZ), :] = total
        return carry

    lax.fori_loop(0, COLS, gather_rows, 0)
    for w in range(NZ):
        zsend[w % 4, w // 4] = acc[pl.ds(w, COLS, stride=NZ), :].astype(BF16)

    core = s % 2
    hubs = (off(z + 12 * core, 2, NZ), off(z, 1, NZ), off(z, -1, NZ))

    def hub_copy(j, p):
        return remote(zsend.at[p % 4], hub_in.at[j], s_sem.at[5], r_sem.at[5], at_z(p))

    def row_copy(j, p):
        return remote(hub_out.at[p // 4], zrecv.at[j], s_sem.at[6], r_sem.at[6], at_z(p))

    for j in range(3):
        hub_copy(j, hubs[j]).start()

    for m in range(2):
        both = states_v.at[m, pl.ds(1, 2)]
        pltpu.make_async_copy(both, both, w_sem.at[6 + 2 * m]).wait()
    pltpu.make_async_copy(scales_s, scales_s, w_sem.at[9]).wait()
    own_up()
    grad_send(1, 0, 1, 4, 5)
    adam(1, y)
    own_down()
    grad_send(0, 0, 1, 4, 5)
    adam(0, y)

    arrived(hub_in, r_sem.at[5])
    for w in range(4):
        part = zsend[z % 4, w].astype(F32)
        for j in range(3):
            part = part + hub_in[j, w].astype(F32)
        hub_out[w] = part.astype(BF16)
    for j in (2, 1, 3):
        row_copy(j, off(z, 4 * j, NZ)).start()

    grad_back(1, 0)
    grad_send(1, 2)
    grad_back(1, 1)
    grad_send(1, 3)
    grad_back(1, 4)
    adam(1, left)
    grad_back(1, 5)
    adam(1, right)
    grad_back(0, 0)
    grad_send(0, 2)
    grad_back(0, 1)
    grad_send(0, 3)
    grad_back(0, 4)
    adam(0, left)
    grad_back(0, 5)
    adam(0, right)
    grad_back(1, 2)
    grad_back(1, 3)
    adam(1, across)
    arrived(hub_out.at[pl.ds(0, 3)], r_sem.at[6])
    row = hub_out[z // 4].astype(F32)
    for j in (1, 2, 3):
        row = row + zrecv[j].astype(F32)
    row = row * valid
    for i in range(COLS):
        layer_ref[0:1, i * BLK : (i + 1) * BLK] = row[i : i + 1, :].astype(BF16)
    layer_out = pltpu.make_async_copy(layer_ref, layer_hbm, w_sem.at[0])
    layer_out.start()
    left_here(hub_in, s_sem.at[5])
    left_here(hub_out.at[pl.ds(0, 3)], s_sem.at[6])
    left_here(cbuf.at[pl.ds(0, NS - 1)], s_sem.at[4])
    left_here(ypick.at[pl.ds(0, NY - 1)], s_sem.at[7])
    left_here(yact.at[pl.ds(0, NY - 1)], s_sem.at[8])
    left_here(grecv, s_sem.at[11])
    left_here(gscale_in, s_sem.at[12])
    grad_back(0, 2)
    grad_back(0, 3)
    adam(0, across)
    scale_out = [pltpu.make_async_copy(scales_v.at[i], new_scales_hbm[i], w_sem.at[1]) for i in range(4)]
    for copy in scale_out:
        copy.start()
    left_here(gsum.at[:, pl.ds(0, 3)], s_sem.at[9])
    left_here(gsum_scale.at[:, pl.ds(0, 3)], s_sem.at[10])
    layer_out.wait()
    pltpu.make_async_copy(states_v, states_v, o_sem).wait()
    pltpu.make_async_copy(scales_v, scales_v, w_sem.at[1]).wait()


def deliver_kernel(*refs):
    n = 11
    held, in_sem, out_sem = refs[2 * n : 3 * n], refs[3 * n], refs[3 * n + 1]
    parts = []
    for i in range(n):
        if len(refs[i].shape) == 3:
            parts += [(i, pl.ds(0, K // 2)), (i, pl.ds(K // 2, K // 2))]
        else:
            parts.append((i, pl.ds(0, refs[i].shape[0])))
    loads = [pltpu.make_async_copy(refs[i].at[at], held[i].at[at], in_sem.at[j]) for j, (i, at) in enumerate(parts)]
    stores = [
        pltpu.make_async_copy(held[i].at[at], refs[n + i].at[at], out_sem.at[i]) for i, at in parts
    ]
    for load in loads:
        load.start()
    for load, store in zip(loads, stores):
        load.wait()
        store.start()
    for i in range(n):
        pltpu.make_async_copy(held[i], refs[n + i], out_sem.at[i]).wait()


def exchange(tokens, cotangent, counts, up_cols, down_rows, up, down):
    hbm = pl.BlockSpec(memory_space=pltpu.HBM)
    free = pl.BlockSpec(memory_space=pl.ANY)
    dma = pltpu.SemaphoreType.DMA
    (uw, um, ums, us, uss) = up
    (dw, dm, dms, ds, dss) = down
    big = jax.ShapeDtypeStruct((K, BLK, BLK), BF16)
    small = jax.ShapeDtypeStruct((GROUPS, K), F32)
    shapes = (jax.ShapeDtypeStruct((1, D), BF16),) + (big,) * 6 + (small,) * 4
    results = pl.pallas_call(
        exchange_kernel,
        out_shape=shapes,
        in_specs=[hbm] * 15,
        out_specs=(free,) * 11,
        scratch_shapes=[
            pltpu.VMEM((1, D), BF16),
            pltpu.VMEM((1, D), BF16),
            pltpu.SMEM((1,), jnp.int32),
            pltpu.SMEM((1, K), jnp.int32),
            pltpu.SMEM((1, K), jnp.int32),
            pltpu.VMEM((1, D), BF16),
            pltpu.VMEM((2, 3, K, BLK, BLK), BF16),
            pltpu.SMEM((4, GROUPS, K), F32),
            pltpu.VMEM((4, GROUPS, K), F32),
            pltpu.VMEM((NZ, 2 * COLS, BLK), BF16),
            pltpu.VMEM((2 * COLS, BLK), F32),
            pltpu.VMEM((2, COLS, NZ, BLK), F32),
            pltpu.VMEM((NS, 8, BLK), jnp.int32),
            pltpu.VMEM((NY, 8, BLK), jnp.int32),
            pltpu.SMEM((NS, 8, BLK), jnp.int32),
            pltpu.VMEM((2, NS, K, QROWS, BLK), BF16),
            pltpu.VMEM((2, NS, K, QROWS, BLK), BF16),
            pltpu.VMEM((NS, K, QROWS, BLK), BF16),
            pltpu.VMEM((NS, K + 1, QROWS, BLK), BF16),
            pltpu.VMEM((COLS * NZ, BLK), F32),
            pltpu.VMEM((4, 4, COLS, BLK), BF16),
            pltpu.VMEM((3, 4, COLS, BLK), BF16),
            pltpu.VMEM((4, COLS, BLK), BF16),
            pltpu.VMEM((4, COLS, BLK), BF16),
            pltpu.VMEM((NY, NS, 4, QROWS, BLK), BF16),
            pltpu.VMEM((NY, ROWS, BLK), BF16),
            pltpu.VMEM((NY, 2, 2, BLK, BLK), jnp.int16),
            pltpu.VMEM((NY, 2, 8, BLK), F32),
            pltpu.VMEM((2, 2, BLK, BLK), jnp.int16),
            pltpu.VMEM((2, 8, BLK), F32),
            pltpu.VMEM((6, 2, BLK, BLK), jnp.int16),
            pltpu.VMEM((6, 8, BLK), F32),
            pltpu.VMEM((2, NY, 2, 2, BLK, BLK), jnp.int16),
            pltpu.VMEM((2, NY, 2, 8, BLK), F32),
            dma((10,)),
            dma,
            dma,
            dma((2, 4)),
            dma((13,)),
            dma((15,)),
            dma((2, 12)),
        ],
        compiler_params=pltpu.CompilerParams(
            collective_id=1, has_side_effects=True, vmem_limit_bytes=60 << 20
        ),
        cost_estimate=pl.CostEstimate(flops=400_000_000, bytes_accessed=8 << 20, transcendentals=1_000_000),
        name="exchange",
    )(
        tokens,
        cotangent,
        counts,
        up_cols,
        down_rows,
        dw,
        dm,
        ds,
        uw,
        um,
        us,
        dms.T,
        dss.T,
        ums.T,
        uss.T,
    )
    results = pl.pallas_call(
        deliver_kernel,
        out_shape=shapes,
        in_specs=[free] * 11,
        out_specs=(hbm,) * 11,
        scratch_shapes=[pltpu.VMEM(a.shape, a.dtype) for a in shapes] + [dma((17,)), dma((11,))],
        compiler_params=pltpu.CompilerParams(vmem_limit_bytes=60 << 20),
        name="deliver",
    )(*results)
    (layer, ndw, ndm, nds, nuw, num, nus, ndms, ndss, nums, nuss) = results
    return (layer, nuw, num, nums.T, nus, nuss.T, ndw, ndm, ndms.T, nds, ndss.T)


def per_device(
    tokens,
    counts,
    up_blocks,
    up_cols,
    down_blocks,
    down_rows,
    cotangent,
    up_moment,
    up_moment_scale,
    up_second,
    up_second_scale,
    down_moment,
    down_moment_scale,
    down_second,
    down_second_scale,
):
    return exchange(
        tokens,
        cotangent,
        counts,
        up_cols,
        down_rows,
        (up_blocks, up_moment, up_moment_scale, up_second, up_second_scale),
        (down_blocks, down_moment, down_moment_scale, down_second, down_second_scale),
    )


def solution(mesh):
    spread = P(("dp", "mp"), None)
    blocks = P("mp", None, None)
    table = P("mp", None)
    side = (blocks, blocks, table, blocks, table)
    return jax.shard_map(
        per_device,
        mesh=mesh,
        in_specs=(spread, P("dp"), blocks, table, blocks, table, spread)
        + (blocks, table, blocks, table) * 2,
        out_specs=(spread,) + side + side,
        check_vma=False,
    )
```
